32 devices in a mesh: row: 8 (over z, x), col: 4 (over y, core).
Axes of the slice: x: 2, y: 2, z: 4, core: 2. Of those that a mesh axis runs over, the one named last changes fastest.
Arguments:
- inputs: bfloat16 [640, 12288], P('row', 'col'), may hold values from -6 to 6
- pre_act: bfloat16 [640, 24576], P('col', 'row'), may hold values from -6 to 6
- out_grad: bfloat16 [640, 12288], P('row', 'col'), may hold values from -6 to 6
- token_valid: int32 [640], P('row'), may hold values 0 or 1
- poison: int32 [8, 4], P('row', 'col'), may hold values 0 or 1
- w_up: bfloat16 [12288, 24576], P('col', 'row'), may hold values from -0.0546875 to 0.0546875
- w_down: bfloat16 [24576, 12288], P('row', 'col'), may hold values from -0.0390625 to 0.0390625
Outputs:
- input_grad: bfloat16 [640, 12288], P('row', 'col')
- grad_up: bfloat16 [12288, 24576], P('col', 'row')
- grad_down: bfloat16 [24576, 12288], P('row', 'col')
The draws below stay inside these ranges and needn't reach their ends.
All inputs are finite; a program needn't handle non-finite values. No bound on the sum of `token_valid` or of `poison` on one device may be relied on, other than what follows from the above.
Results may differ from the reference program's by a relative error of at most 0.0051.
Values may be sent and summed in bfloat16 or wider, within the bound.
No kernel may reach another device: no remote copies, remote signals or barrier semaphores. Data moves between devices by JAX's collectives and lax.ppermute only.
A program may use at most 384 MiB of HBM per device.

```python
import math
import jax
import jax.numpy as jnp

D = 12288
FF = 24576
TOKENS = 640
N_ROW = 8
N_COL = 4


def place_ends(drawn, own_key, low, largest):
    index_at = [jax.random.randint(jax.random.fold_in(own_key, axis), (), 0, length) for axis, length in enumerate(drawn.shape)]
    widest = drawn.shape.index(max(drawn.shape))
    neighbour = index_at[:widest] + [(index_at[widest] + 1) % drawn.shape[widest]] + index_at[widest + 1:]
    return drawn.at[tuple(index_at)].set(low).at[tuple(neighbour)].set(largest)


def level_of(rng, extent, cuts, low, top_value):
    factor_of, own = 1.0, jax.random.fold_in(rng, 6)
    for dim, shards_of in cuts:
        heights = jnp.exp(jax.random.uniform(jax.random.fold_in(own, dim), (shards_of,), jnp.float32, low / len(cuts), top_value / len(cuts)))
        factor_of = factor_of * jnp.repeat(heights, extent[dim] // shards_of).reshape([-1 if axis == dim else 1 for axis in range(len(extent))])
    return factor_of


def gaussian(own_key, extent, width, reach, shards=(), dtype=jnp.bfloat16):
    drawn = width * jax.random.normal(own_key, extent, jnp.float32)
    if shards:
        drawn = drawn * level_of(own_key, extent, shards, -0.22, 0.18)
    return jnp.clip(drawn, -reach, reach).astype(dtype)


def setup_inputs(seed: int = 0) -> dict:
    seeds = jax.random.split(jax.random.key(seed), 8)
    inputs = gaussian(seeds[0], (TOKENS, D), 1.0, 6.0, ((0, 8), (1, 4)))
    pre_act = gaussian(seeds[1], (TOKENS, FF), 1.0, 6.0, ((0, 4), (1, 8)))
    out_grad = gaussian(seeds[2], (TOKENS, D), 1.0, 6.0, ((0, 8), (1, 4)))
    token_valid = place_ends((jax.random.randint(seeds[3], (TOKENS,), 0, 4) < 3).astype(jnp.int32), jax.random.fold_in(seeds[3], 1), 0, 1)
    poison = place_ends((jax.random.randint(seeds[4], (N_ROW, N_COL), 0, 4) < 1).astype(jnp.int32), jax.random.fold_in(seeds[4], 1), 0, 1)
    w_up = gaussian(seeds[5], (D, FF), D ** -0.5, 0.0546875, ((0, 4), (1, 8)))
    w_down = gaussian(seeds[6], (FF, D), FF ** -0.5, 0.0390625, ((0, 8), (1, 4)))
    return {"inputs": inputs, "pre_act": pre_act, "out_grad": out_grad, "token_valid": token_valid, "poison": poison, "w_up": w_up, "w_down": w_down}


def gelu_value(hval):
    inner = math.sqrt(2.0 / math.pi) * (hval + 0.044715 * hval * hval * hval)
    return 0.5 * hval * (1.0 + jnp.tanh(inner))

def gelu_slope(hval):
    factor = math.sqrt(2.0 / math.pi)
    tanh_part = jnp.tanh(factor * (hval + 0.044715 * hval * hval * hval))
    return 0.5 * (1.0 + tanh_part) + 0.5 * hval * (1.0 - tanh_part * tanh_part) * factor * (1.0 + 3.0 * 0.044715 * hval * hval)

def reference(inputs, pre_act, out_grad, token_valid, poison, w_up, w_down):
    masked = out_grad * token_valid.astype(jnp.bfloat16)[:, None]
    token_total = jnp.maximum(jnp.sum(token_valid.astype(jnp.float32)), 1.0)
    act_grad = jnp.dot(masked, w_down.T, preferred_element_type=jnp.float32)
    hval = pre_act.astype(jnp.float32)
    activation = gelu_value(hval).astype(jnp.bfloat16)
    hidden_grad = (act_grad * gelu_slope(hval)).astype(jnp.bfloat16)
    raw_down = jnp.dot(activation.T, masked, preferred_element_type=jnp.float32) / token_total
    raw_up = jnp.dot(inputs.T, hidden_grad, preferred_element_type=jnp.float32) / token_total
    input_grad = (jnp.dot(hidden_grad, w_up.T, preferred_element_type=jnp.float32) / token_total).astype(jnp.bfloat16)
    keep_blocks = 1.0 - poison.astype(jnp.float32)
    up_blocks = raw_up.reshape(N_COL, D // N_COL, N_ROW, FF // N_ROW) * keep_blocks.T[:, None, :, None]
    down_blocks = raw_down.reshape(N_ROW, FF // N_ROW, N_COL, D // N_COL) * keep_blocks[:, None, :, None]
    squares = jnp.sum(up_blocks * up_blocks) + jnp.sum(down_blocks * down_blocks)
    flagged = jnp.sum(poison.astype(jnp.float32))
    block_count = float(N_ROW * N_COL)
    estimate = squares * block_count / jnp.maximum(block_count - flagged, 1.0)
    limit = 0.25 * math.sqrt(FF * D / TOKENS)
    clip_factor = jnp.minimum(1.0, limit / jnp.sqrt(estimate + 1e-06))
    grad_up = (up_blocks * clip_factor).reshape(D, FF).astype(jnp.bfloat16)
    grad_down = (down_blocks * clip_factor).reshape(FF, D).astype(jnp.bfloat16)
    return (input_grad, grad_up, grad_down)
```

```python
import math

import jax
import jax.numpy as jnp
import numpy as np
from jax import lax
from jax.sharding import PartitionSpec as P

F32 = jnp.float32
BF16 = jnp.bfloat16
LAST = (((1,), (1,)), ((), ()))
FIRST = (((0,), (0,)), ((), ()))
FACTOR = math.sqrt(2.0 / math.pi)


def gelu_value(hval):
    inner = FACTOR * (hval + 0.044715 * hval * hval * hval)
    return 0.5 * hval * (1.0 + jnp.tanh(inner))


def gelu_slope(hval):
    tanh_part = jnp.tanh(FACTOR * (hval + 0.044715 * hval * hval * hval))
    return 0.5 * (1.0 + tanh_part) + 0.5 * hval * (1.0 - tanh_part * tanh_part) * FACTOR * (
        1.0 + 3.0 * 0.044715 * hval * hval
    )


def line_plan(length):
    order = []
    for z in range(length):
        prefer = -1 if z % 2 else 1
        others = [s for s in range(length) if s != z]
        others.sort(key=lambda s: (abs(s - z), -prefer * (s - z)))
        order.append([z] + others)
    groups = {}
    for z in range(length):
        for slot in range(1, length):
            shard = order[z][slot]
            near = z - 1 if shard < z else z + 1
            from_slot = order[near].index(shard)
            side = 0
            while True:
                pairs = groups.setdefault((abs(shard - z), slot, from_slot, side), [])
                if all(near != source for source, _ in pairs):
                    pairs.append((near, z))
                    break
                side += 1
    hops = [(key[0], key[1], key[2], groups[key]) for key in sorted(groups)]
    return order, hops


def on_row(pairs):
    return [(2 * a + x, 2 * b + x) for a, b in pairs for x in range(2)]


def swap(value, axis, bit):
    size = lax.axis_size(axis)
    return lax.ppermute(value, axis, [(i, i ^ bit) for i in range(size)])


def member(z, nodes):
    return sum((z == node).astype(jnp.int32) for node in nodes) > 0


def line_gather(own, z, length, hops):
    slots = [own] + [None] * (length - 1)
    arrived = {(0, 0): own}
    for time, slot, from_slot, pairs in hops:
        got = lax.ppermute(arrived[(time - 1, from_slot)], "row", on_row(pairs))
        here = member(z, [b for _, b in pairs])
        for table, key in ((arrived, (time, slot)), (slots, slot)):
            before = table[key] if isinstance(table, list) else table.get(key)
            merged = got if before is None else jnp.where(here, got, before)
            table[key] = merged
    return slots


def line_reduce(parts, hops):
    sums = list(parts)
    for _, slot, from_slot, pairs in reversed(hops):
        got = lax.ppermute(
            sums[slot].astype(BF16), "row", on_row([(b, a) for a, b in pairs])
        )
        sums[from_slot] = sums[from_slot] + got.astype(F32)
    return sums[0]


def after(value, event):
    return lax.optimization_barrier((value, event))[0]


def on_device(inputs, pre_act, out_grad, token_valid, poison, w_up, w_down):
    n_row = lax.axis_size("row")
    n_col = lax.axis_size("col")
    rows = inputs.shape[0]
    length = n_row // 2
    order, hops = line_plan(length)
    row, col = lax.axis_index("row"), lax.axis_index("col")
    z, x, core = row // 2, row % 2, col % 2
    first_core = core == 0

    def split(mine, theirs):
        return jnp.where(first_core, mine, theirs), jnp.where(first_core, theirs, mine)

    def halves(mine, theirs):
        return jnp.concatenate(split(mine, theirs), axis=0)

    masked = out_grad * token_valid.astype(BF16)[:, None]
    masked_mine = line_gather(masked, z, length, hops)
    masked_theirs = [swap(part, "row", 1) for part in masked_mine]
    masked_slots = [halves(a, b) for a, b in zip(masked_mine, masked_theirs)]

    inputs_late = after(inputs, masked_mine[-1])
    inputs_mine = line_gather(inputs_late, z, length, hops)
    inputs_theirs = [swap(part, "row", 1) for part in inputs_mine]
    inputs_all = jnp.concatenate(
        [halves(a, b) for a, b in zip(inputs_mine, inputs_theirs)], axis=0
    )
    masked_all = jnp.concatenate(masked_slots, axis=0)

    bits = []
    bit = n_col // 2
    while bit:
        bits.append(bit)
        bit //= 2
    pieces = [pre_act]
    for bit in bits:
        pieces = pieces + [swap(piece, "col", bit) for piece in pieces]
    gathered = jnp.concatenate(pieces, axis=0)
    per_col = n_row // n_col
    table = jnp.asarray(np.array(order, np.int32))

    def hidden_rows(slot, half):
        which = 2 * table[z, slot] + (x ^ core ^ half)
        apart = (which // per_col) ^ col
        place = sum(((apart // bit) % 2) << i for i, bit in enumerate(bits))
        start = (place * per_col + which % per_col) * rows
        return lax.dynamic_slice_in_dim(gathered, start, rows, axis=0)

    pre_halves = [(hidden_rows(slot, 0), hidden_rows(slot, 1)) for slot in range(length)]
    act_all = gelu_value(
        jnp.concatenate([half for pair in pre_halves for half in pair], axis=0).astype(F32)
    ).astype(BF16)

    hidden_slots = []
    for slot in range(length):
        partial = lax.dot_general(
            masked_slots[slot], w_down, LAST, preferred_element_type=F32
        )
        other = swap(partial[rows:].astype(BF16), "col", 1)
        total = partial[:rows] + other.astype(F32)
        for bit in reversed(bits[:-1]):
            total = total + swap(total.astype(BF16), "col", bit).astype(F32)
        hidden = (total * gelu_slope(pre_halves[slot][0].astype(F32))).astype(BF16)
        hidden_slots.append(jnp.concatenate([hidden, swap(hidden, "col", 1)], axis=0))
    hidden_all = jnp.concatenate(hidden_slots, axis=0)

    sums = [None] * length
    for slot in reversed(range(length)):
        partial = lax.dot_general(
            hidden_slots[slot], w_up, LAST, preferred_element_type=F32
        )
        mine, theirs = split(partial[:rows], partial[rows:])
        sums[slot] = mine + swap(theirs.astype(BF16), "row", 1).astype(F32)
    input_sum = line_reduce(sums, hops)

    def gram(value):
        return lax.dot_general(value, value, LAST, preferred_element_type=F32)

    square_term = jnp.sum(gram(act_all) * gram(masked_all)) + jnp.sum(
        gram(hidden_all) * gram(inputs_all)
    )
    flag_value = poison[0, 0].astype(F32)
    keep_block = 1.0 - flag_value
    count_term = jnp.where(col == 0, jnp.sum(token_valid.astype(F32)), 0.0)
    scalars = jnp.stack([count_term, keep_block * square_term, flag_value])
    for axis, size in (("col", n_col), ("row", n_row)):
        bit = 1
        while bit < size:
            scalars = scalars + swap(scalars, axis, bit)
            bit *= 2
    count_all, square_all, flag_all = scalars[0], jnp.maximum(scalars[1], 0.0), scalars[2]

    token_total = jnp.maximum(count_all, 1.0)
    squares = square_all / (token_total * token_total)
    block_count = float(n_row * n_col)
    estimate = squares * block_count / jnp.maximum(block_count - flag_all, 1.0)
    total_tokens = rows * n_row
    model_width = w_up.shape[0] * n_col
    hidden_width = w_up.shape[1] * n_row
    limit = 0.25 * math.sqrt(hidden_width * model_width / total_tokens)
    clip_factor = jnp.minimum(1.0, limit / jnp.sqrt(estimate + 1e-06))
    scale = keep_block * clip_factor / token_total
    grad_up = lax.dot_general(inputs_all, hidden_all, FIRST, preferred_element_type=F32)
    grad_down = lax.dot_general(act_all, masked_all, FIRST, preferred_element_type=F32)
    return (
        (input_sum / token_total).astype(BF16),
        (grad_up * scale).astype(BF16),
        (grad_down * scale).astype(BF16),
    )


def solution(mesh):
    placed = (
        P("row", "col"),
        P("col", "row"),
        P("row", "col"),
        P("row"),
        P("row", "col"),
        P("col", "row"),
        P("row", "col"),
    )
    return jax.shard_map(
        on_device,
        mesh=mesh,
        in_specs=placed,
        out_specs=(P("row", "col"), P("col", "row"), P("row", "col")),
        check_vma=False,
    )
```

```python
import functools
import math

import jax
import jax.numpy as jnp
from jax import lax
from jax.experimental import pallas as pl
from jax.experimental.pallas import tpu as pltpu
from jax.sharding import PartitionSpec as P

F32 = jnp.float32
BF16 = jnp.bfloat16
LAST = (((1,), (1,)), ((), ()))
FIRST = (((0,), (0,)), ((), ()))
FACTOR = math.sqrt(2.0 / math.pi)
TILE = 256
VMEM_LIMIT = 56 * 1024 * 1024


def swap(value, axis, bit):
    size = lax.axis_size(axis)
    return lax.ppermute(value, axis, [(i, i ^ bit) for i in range(size)])


def call(kernel, grid, in_specs, out_specs, out_shape, scratch, cost):
    flops, moved, slow = cost
    return pl.pallas_call(
        kernel,
        grid_spec=pltpu.PrefetchScalarGridSpec(
            num_scalar_prefetch=1,
            grid=grid,
            in_specs=in_specs,
            out_specs=out_specs,
            scratch_shapes=scratch,
        ),
        out_shape=out_shape,
        compiler_params=pltpu.CompilerParams(
            dimension_semantics=("arbitrary",), vmem_limit_bytes=VMEM_LIMIT
        ),
        cost_estimate=pl.CostEstimate(
            flops=flops, bytes_accessed=moved, transcendentals=slow
        ),
    )


class Rows:
    def __init__(self, arrays, places, length, rows, by_core=False):
        self.arrays, self.places = arrays, places
        self.length, self.rows, self.by_core = length, rows, by_core

    def specs(self, width, index):
        return [pl.BlockSpec((a.shape[0], width), index) for a in self.arrays]

    def fill(self, target, refs, core):
        for ref, (half, first, count) in zip(refs, self.places):
            base = (half ^ core if self.by_core else half) * (self.length * self.rows)
            for node in range(self.length):
                start = base + node * self.rows + first
                if self.by_core:
                    start = pl.multiple_of(start, 16)
                target[pl.ds(start, count), :] = ref[node * count : (node + 1) * count, :]


def whole_index(i, flags):
    return (0, 0)


def column_index(i, flags):
    return (0, i)


def gelu_all(pieces, offsets, flags, per_col, length, rows):
    width = pieces[0].shape[1]
    tile = 2 * TILE
    tokens = 2 * length * rows

    def kernel(flags_ref, *refs):
        ins, (act_ref, slope_ref) = refs[: len(pieces)], refs[len(pieces) :]
        x, core, col = flags_ref[0], flags_ref[1], flags_ref[2]
        for ref, offset in zip(ins, offsets):
            for part in range(per_col):
                row = (col ^ offset) * per_col + part
                node, half = row // 2, (row % 2) ^ x
                hval = ref[part * rows : (part + 1) * rows, :].astype(F32)
                tanh_part = jnp.tanh(FACTOR * (hval + 0.044715 * hval * hval * hval))
                start = pl.multiple_of((half * length + node) * rows, 16)
                act_ref[pl.ds(start, rows), :] = (0.5 * hval * (1.0 + tanh_part)).astype(BF16)

                @pl.when(half == core)
                def _():
                    slope_ref[pl.ds(pl.multiple_of(node * rows, 16), rows), :] = 0.5 * (
                        1.0 + tanh_part
                    ) + 0.5 * hval * (1.0 - tanh_part * tanh_part) * FACTOR * (
                        1.0 + 3.0 * 0.044715 * hval * hval
                    )

    return call(
        kernel,
        (width // tile,),
        [pl.BlockSpec((p.shape[0], tile), column_index) for p in pieces],
        [
            pl.BlockSpec((tokens, tile), column_index),
            pl.BlockSpec((tokens // 2, tile), column_index),
        ],
        [
            jax.ShapeDtypeStruct((tokens, width), BF16),
            jax.ShapeDtypeStruct((tokens // 2, width), F32),
        ],
        [],
        (30 * tokens * width, 6 * tokens * width, tokens * width),
    )(flags, *pieces)


def act_grad_part(mine, theirs, w_down, flags):
    count, depth = mine.shape
    width = w_down.shape[0]

    def kernel(flags_ref, mine_ref, theirs_ref, w_ref, keep_ref, send_ref, both):
        @pl.when(pl.program_id(0) == 0)
        def _():
            core = flags_ref[1]
            both[pl.ds(pl.multiple_of(core * count, 16), count), :] = mine_ref[...]
            both[pl.ds(pl.multiple_of((1 - core) * count, 16), count), :] = theirs_ref[...]

        product = lax.dot_general(both[...], w_ref[...], LAST, preferred_element_type=F32)
        keep_ref[...] = product[:count]
        send_ref[...] = product[count:].astype(BF16)

    return call(
        kernel,
        (width // TILE,),
        [
            pl.BlockSpec((count, depth), whole_index),
            pl.BlockSpec((count, depth), whole_index),
            pl.BlockSpec((TILE, depth), lambda i, flags: (i, 0)),
        ],
        [pl.BlockSpec((count, TILE), column_index)] * 2,
        [
            jax.ShapeDtypeStruct((count, width), F32),
            jax.ShapeDtypeStruct((count, width), BF16),
        ],
        [pltpu.VMEM((2 * count, depth), BF16)],
        (4 * count * depth * width, 2 * depth * width + 10 * count * width, 0),
    )(flags, mine, theirs, w_down)


def input_part(hidden, w_up, first, width, flags):
    depth = w_up.shape[1]
    half = hidden.length * hidden.rows
    n = len(hidden.arrays)

    def kernel(flags_ref, *refs):
        w_ref, mine_ref, theirs_ref, both = refs[n:]

        @pl.when(pl.program_id(0) == 0)
        def _():
            hidden.fill(both, refs[:n], flags_ref[1])

        product = lax.dot_general(both[...], w_ref[...], LAST, preferred_element_type=F32)
        mine_ref[...] = product[:half]
        theirs_ref[...] = product[half:].astype(BF16)

    return call(
        kernel,
        (width // TILE,),
        hidden.specs(depth, whole_index)
        + [pl.BlockSpec((TILE, depth), lambda i, flags: (first // TILE + i, 0))],
        [pl.BlockSpec((half, TILE), column_index)] * 2,
        [
            jax.ShapeDtypeStruct((half, width), F32),
            jax.ShapeDtypeStruct((half, width), BF16),
        ],
        [pltpu.VMEM((2 * half, depth), BF16)],
        (4 * half * depth * width, 2 * depth * width + 4 * half * (depth + 2 * width), 0),
    )(flags, *hidden.arrays, w_up)


def gram_inner(left, right, flags):
    width = left.arrays[0].shape[1]
    tile = 2 * TILE if width % (2 * TILE) == 0 else TILE
    tokens = 2 * left.length * left.rows
    n, m = len(left.arrays), len(right.arrays)
    steps = width // tile

    def kernel(flags_ref, *refs):
        out_ref, left_all, right_all, left_gram, right_gram = refs[n + m :]
        step, core = pl.program_id(0), flags_ref[1]
        left.fill(left_all, refs[:n], core)
        right.fill(right_all, refs[n : n + m], core)

        @pl.when(step == 0)
        def _():
            left_gram[...] = jnp.zeros_like(left_gram)
            right_gram[...] = jnp.zeros_like(right_gram)

        for rows, total in ((left_all, left_gram), (right_all, right_gram)):
            total[...] += lax.dot_general(
                rows[...], rows[...], LAST, preferred_element_type=F32
            )

        @pl.when(step == steps - 1)
        def _():
            out_ref[...] = jnp.sum(left_gram[...] * right_gram[...], axis=0, keepdims=True)

    gram = pltpu.VMEM((tokens, tokens), F32)
    out = call(
        kernel,
        (steps,),
        left.specs(tile, column_index) + right.specs(tile, column_index),
        pl.BlockSpec((1, tokens), whole_index),
        jax.ShapeDtypeStruct((1, tokens), F32),
        [pltpu.VMEM((tokens, tile), BF16)] * 2 + [gram] * 2,
        (4 * tokens * tokens * width, 4 * tokens * width, 0),
    )(flags, *left.arrays, *right.arrays)
    return jnp.sum(out)


def gradient(left, right, scale, flags):
    width, right_width = left.arrays[0].shape[1], right.arrays[0].shape[1]
    tokens = 2 * left.length * left.rows
    n, m = len(left.arrays), len(right.arrays)

    def kernel(flags_ref, scale_ref, *refs):
        out_ref, left_all, right_all = refs[n + m :]
        core = flags_ref[1]

        @pl.when(pl.program_id(0) == 0)
        def _():
            right.fill(right_all, refs[n : n + m], core)

        left.fill(left_all, refs[:n], core)
        product = lax.dot_general(
            left_all[...], right_all[...], FIRST, preferred_element_type=F32
        )
        out_ref[...] = (product * scale_ref[0, 0]).astype(BF16)

    return call(
        kernel,
        (width // TILE,),
        [pl.BlockSpec(memory_space=pltpu.SMEM)]
        + left.specs(TILE, column_index)
        + right.specs(right_width, whole_index),
        pl.BlockSpec((TILE, right_width), lambda i, flags: (i, 0)),
        jax.ShapeDtypeStruct((width, right_width), BF16),
        [pltpu.VMEM((tokens, TILE), BF16), pltpu.VMEM((tokens, right_width), BF16)],
        (
            2 * tokens * width * right_width,
            2 * width * right_width + 2 * tokens * (width + right_width),
            0,
        ),
    )(flags, scale.reshape(1, 1), *left.arrays, *right.arrays)


def row_chunks(rows):
    units, left = rows // 16, rows % 16
    if left or units < 3:
        return [(0, rows)]
    sizes = [units // 3, (units - units // 3) // 2]
    sizes.append(units - sum(sizes))
    firsts = [0, sizes[0], sizes[0] + sizes[1]]
    return [(16 * first, 16 * size) for first, size in zip(firsts, sizes)]


def on_device(inputs, pre_act, out_grad, token_valid, poison, w_up, w_down):
    n_row = lax.axis_size("row")
    n_col = lax.axis_size("col")
    rows = inputs.shape[0]
    length = n_row // 2
    row, col = lax.axis_index("row"), lax.axis_index("col")
    x, core = row % 2, col % 2
    flags = jnp.stack([x, core, col]).astype(jnp.int32)
    lines = [[2 * node + side for node in range(length)] for side in range(2)]
    bits = []
    bit = n_col // 2
    while bit:
        bits.append(bit)
        bit //= 2

    def along_line(value):
        return lax.all_gather(value, "row", axis=0, tiled=True, axis_index_groups=lines)

    masked = out_grad * token_valid.astype(BF16)[:, None]
    chunks = row_chunks(rows)
    masked_mine = [along_line(masked[a : a + n]) for a, n in chunks]
    masked_theirs = [swap(part, "row", 1) for part in masked_mine]

    pieces, offsets = [pre_act], [0]
    for bit in bits:
        pieces = pieces + [swap(piece, "col", bit) for piece in pieces]
        offsets = offsets + [offset ^ bit for offset in offsets]
    act, slope = gelu_all(pieces, offsets, flags, n_row // n_col, length, rows)
    slope = slope.reshape(length, rows, -1)

    kept, sent = [], []
    for (first, count), mine, theirs in zip(chunks, masked_mine, masked_theirs):
        keep, send = act_grad_part(mine, theirs, w_down, flags)
        total = keep + swap(send, "col", 1).astype(F32)
        for bit in reversed(bits[:-1]):
            total = total + swap(total.astype(BF16), "col", bit).astype(F32)
        slope_part = slope[:, first : first + count].reshape(total.shape)
        hidden = (total * slope_part).astype(BF16)
        kept.append(hidden)
        sent.append(swap(hidden, "col", 1))

    width = inputs.shape[1] // 2
    inputs_mine = [along_line(inputs[:, i * width : (i + 1) * width]) for i in range(2)]
    inputs_theirs = [swap(part, "row", 1) for part in inputs_mine]

    places = [(half, first, count) for half in range(2) for first, count in chunks]
    full = [(0, 0, rows), (1, 0, rows)]
    hidden_all = Rows(kept + sent, places, length, rows, by_core=True)
    masked_all = Rows(masked_mine + masked_theirs, places, length, rows)
    act_all = Rows([act[: length * rows], act[length * rows :]], full, length, rows)
    inputs_all = [
        Rows(list(pair), full, length, rows) for pair in zip(inputs_mine, inputs_theirs)
    ]
    inputs_whole = Rows(
        [jnp.concatenate(inputs_mine, axis=1), jnp.concatenate(inputs_theirs, axis=1)],
        full,
        length,
        rows,
    )
    del inputs_all

    model = w_up.shape[0]
    parts = 3 if model % (3 * TILE) == 0 else 1
    step = model // parts
    input_sums = []
    for part in range(parts):
        mine, theirs = input_part(hidden_all, w_up, part * step, step, flags)
        pair = (mine + swap(theirs, "row", 1).astype(F32)).astype(BF16)
        input_sums.append(
            lax.psum_scatter(
                pair, "row", scatter_dimension=0, axis_index_groups=lines, tiled=True
            )
        )

    square_term = gram_inner(act_all, masked_all, flags) + gram_inner(
        inputs_whole, hidden_all, flags
    )
    flag_value = poison[0, 0].astype(F32)
    keep_block = 1.0 - flag_value
    count_term = jnp.where(col == 0, jnp.sum(token_valid.astype(F32)), 0.0)
    scalars = jnp.stack([count_term, keep_block * square_term, flag_value])
    for axis, size in (("col", n_col), ("row", n_row)):
        bit = 1
        while bit < size:
            scalars = scalars + swap(scalars, axis, bit)
            bit *= 2
    count_all, square_all, flag_all = scalars[0], jnp.maximum(scalars[1], 0.0), scalars[2]

    token_total = jnp.maximum(count_all, 1.0)
    squares = square_all / (token_total * token_total)
    block_count = float(n_row * n_col)
    estimate = squares * block_count / jnp.maximum(block_count - flag_all, 1.0)
    total_tokens = rows * n_row
    model_width = w_up.shape[0] * n_col
    hidden_width = w_up.shape[1] * n_row
    limit = 0.25 * math.sqrt(hidden_width * model_width / total_tokens)
    clip_factor = jnp.minimum(1.0, limit / jnp.sqrt(estimate + 1e-06))
    scale = keep_block * clip_factor / token_total
    grad_down = gradient(act_all, masked_all, scale, flags)
    grad_up = gradient(inputs_whole, hidden_all, scale, flags)
    input_sum = jnp.concatenate(input_sums, axis=1).astype(F32)
    return (input_sum / token_total).astype(BF16), grad_up, grad_down


def solution(mesh):
    placed = (
        P("row", "col"),
        P("col", "row"),
        P("row", "col"),
        P("row"),
        P("row", "col"),
        P("col", "row"),
        P("row", "col"),
    )
    return jax.shard_map(
        on_device,
        mesh=mesh,
        in_specs=placed,
        out_specs=(P("row", "col"), P("col", "row"), P("row", "col")),
        check_vma=False,
    )
```

```python
import math

import jax
import jax.numpy as jnp
from jax import lax
from jax.experimental import pallas as pl
from jax.experimental.pallas import tpu as pltpu
from jax.sharding import PartitionSpec as P

F32 = jnp.float32
BF16 = jnp.bfloat16
LAST = (((1,), (1,)), ((), ()))
PLAIN = (((1,), (0,)), ((), ()))
FACTOR = math.sqrt(2.0 / math.pi)
TILE = 256
VMEM_LIMIT = 56 * 1024 * 1024


def swap(value, axis, bit):
    size = lax.axis_size(axis)
    return lax.ppermute(value, axis, [(i, i ^ bit) for i in range(size)])


def bits_of(size):
    return [1 << i for i in range(size.bit_length() - 1)]


def turned(index, size):
    return sum(((index // bit) % 2) * (size // 2 // bit) for bit in bits_of(size))


def call(kernel, grid, in_specs, out_specs, out_shape, scratch, cost):
    flops, moved, slow = cost
    return pl.pallas_call(
        kernel,
        grid_spec=pltpu.PrefetchScalarGridSpec(
            num_scalar_prefetch=1,
            grid=grid,
            in_specs=in_specs,
            out_specs=out_specs,
            scratch_shapes=scratch,
        ),
        out_shape=out_shape,
        compiler_params=pltpu.CompilerParams(
            dimension_semantics=("arbitrary",), vmem_limit_bytes=VMEM_LIMIT
        ),
        cost_estimate=pl.CostEstimate(
            flops=flops, bytes_accessed=moved, transcendentals=slow
        ),
    )


def whole_index(i, flags):
    return (0, 0)


def column_index(i, flags):
    return (0, i)


def row_index(i, flags):
    return (i, 0)


def aligned(start):
    return pl.multiple_of(start, 16)


def gelu_all(pre_all, flags, n_row, rows):
    tokens, width = pre_all.shape

    def kernel(flags_ref, pre_ref, act_ref, turn_ref, slope_ref):
        row, core = flags_ref[0], flags_ref[1]
        for source in range(n_row):
            index = row ^ source
            hval = pre_ref[source * rows : (source + 1) * rows, :].astype(F32)
            tanh_part = jnp.tanh(FACTOR * (hval + 0.044715 * hval * hval * hval))
            act_ref[pl.ds(aligned(turned(index, n_row) * rows), rows), :] = (
                0.5 * hval * (1.0 + tanh_part)
            ).astype(BF16)

            @pl.when(index % 2 == core)
            def _():
                slope_ref[pl.ds(aligned((index // 2) * rows), rows), :] = 0.5 * (
                    1.0 + tanh_part
                ) + 0.5 * hval * (1.0 - tanh_part * tanh_part) * FACTOR * (
                    1.0 + 3.0 * 0.044715 * hval * hval
                )

        turn_ref[...] = act_ref[...].T

    return call(
        kernel,
        (width // TILE,),
        [pl.BlockSpec((tokens, TILE), column_index)],
        [
            pl.BlockSpec((tokens, TILE), column_index),
            pl.BlockSpec((TILE, tokens), row_index),
            pl.BlockSpec((tokens // 2, TILE), column_index),
        ],
        [
            jax.ShapeDtypeStruct((tokens, width), BF16),
            jax.ShapeDtypeStruct((width, tokens), BF16),
            jax.ShapeDtypeStruct((tokens // 2, width), F32),
        ],
        [],
        (30 * tokens * width, 8 * tokens * width, tokens * width),
    )(flags, pre_all)


def act_grad_part(mine, theirs, w_down, flags):
    rows, depth = mine[0].shape
    n = len(mine)
    count = n * rows
    padded = -(-2 * count // 128) * 128
    width = w_down.shape[0]

    def kernel(flags_ref, *refs):
        w_ref, keep_ref, send_ref, both, both_turned = refs[2 * n :]

        @pl.when(pl.program_id(0) == 0)
        def _():
            core = flags_ref[1]
            if padded > 2 * count:
                both[2 * count :, :] = jnp.zeros((padded - 2 * count, depth), BF16)
            for i, ref in enumerate(refs[: 2 * n]):
                place = (core if i < n else 1 - core) * count + (i % n) * rows
                both[pl.ds(aligned(place), rows), :] = ref[...]
            both_turned[...] = both[...].T

        product = lax.dot_general(
            w_ref[...], both_turned[...], PLAIN, preferred_element_type=F32
        ).T
        keep_ref[...] = product[:count]
        send_ref[...] = product[count : 2 * count].astype(BF16)

    return call(
        kernel,
        (width // TILE,),
        [pl.BlockSpec((rows, depth), whole_index)] * (2 * n)
        + [pl.BlockSpec((TILE, depth), row_index)],
        [pl.BlockSpec((count, TILE), column_index)] * 2,
        [
            jax.ShapeDtypeStruct((count, width), F32),
            jax.ShapeDtypeStruct((count, width), BF16),
        ],
        [pltpu.VMEM((padded, depth), BF16), pltpu.VMEM((depth, padded), BF16)],
        (4 * count * depth * width, 2 * depth * width + 10 * count * width, 0),
    )(flags, *mine, *theirs, w_down)


def arrange(pieces, places, tokens, rows, flags):
    width = pieces[0].shape[1]
    tile = 2 * TILE if width % (2 * TILE) == 0 else TILE
    n = len(pieces)

    def kernel(flags_ref, *refs):
        out_ref, turn_ref = refs[n:]
        row, core = flags_ref[0], flags_ref[1]
        for ref, blocks in zip(refs[:n], places):
            for k, place in enumerate(blocks):
                out_ref[pl.ds(aligned(place(row, core) * rows), rows), :] = ref[
                    k * rows : (k + 1) * rows, :
                ]
        turn_ref[...] = out_ref[...].T

    return call(
        kernel,
        (width // tile,),
        [pl.BlockSpec((p.shape[0], tile), column_index) for p in pieces],
        [
            pl.BlockSpec((tokens, tile), column_index),
            pl.BlockSpec((tile, tokens), row_index),
        ],
        [
            jax.ShapeDtypeStruct((tokens, width), BF16),
            jax.ShapeDtypeStruct((width, tokens), BF16),
        ],
        [],
        (0, 6 * tokens * width, 0),
    )(flags, *pieces)


def input_part(hidden_turned, w_up, first, width, flags):
    depth, tokens = hidden_turned.shape
    half = tokens // 2

    def kernel(flags_ref, turned_ref, w_ref, mine_ref, theirs_ref):
        product = lax.dot_general(
            w_ref[...], turned_ref[...], PLAIN, preferred_element_type=F32
        ).T
        mine_ref[...] = product[:half]
        theirs_ref[...] = product[half:].astype(BF16)

    return call(
        kernel,
        (width // TILE,),
        [
            pl.BlockSpec((depth, tokens), whole_index),
            pl.BlockSpec((TILE, depth), lambda i, flags: (first // TILE + i, 0)),
        ],
        [pl.BlockSpec((half, TILE), column_index)] * 2,
        [
            jax.ShapeDtypeStruct((half, width), F32),
            jax.ShapeDtypeStruct((half, width), BF16),
        ],
        [],
        (2 * tokens * depth * width, 2 * depth * width + 2 * tokens * depth, 0),
    )(flags, hidden_turned, w_up)


def gram_inner(left, left_turned, right, right_turned, rows, flags):
    pieces = left if left_turned is None else [left, left_turned]
    n = len(pieces)
    tokens, width = right.shape
    tile = 2 * TILE if width % (2 * TILE) == 0 else TILE
    steps = width // tile

    def kernel(flags_ref, *refs):
        right_ref, right_turn_ref, out_ref, left_gram, right_gram = refs[n : n + 5]
        step = pl.program_id(0)

        @pl.when(step == 0)
        def _():
            left_gram[...] = jnp.zeros_like(left_gram)
            right_gram[...] = jnp.zeros_like(right_gram)

        if left_turned is None:
            left_all = refs[n + 5]
            for i, ref in enumerate(refs[:n]):
                left_all[i * rows : (i + 1) * rows, :] = ref[...]
            left_gram[...] += lax.dot_general(
                left_all[...], left_all[...], LAST, preferred_element_type=F32
            )
        else:
            left_gram[...] += lax.dot_general(
                refs[0][...], refs[1][...], PLAIN, preferred_element_type=F32
            )
        right_gram[...] += lax.dot_general(
            right_ref[...], right_turn_ref[...], PLAIN, preferred_element_type=F32
        )

        @pl.when(step == steps - 1)
        def _():
            out_ref[...] = jnp.sum(left_gram[...] * right_gram[...], axis=0, keepdims=True)

    plain = [pl.BlockSpec((tokens, tile), column_index), pl.BlockSpec((tile, tokens), row_index)]
    gram = pltpu.VMEM((tokens, tokens), F32)
    if left_turned is None:
        left_specs = [pl.BlockSpec((rows, tile), column_index)] * n
        extra = [pltpu.VMEM((tokens, tile), BF16)]
    else:
        left_specs, extra = plain, []
    out = call(
        kernel,
        (steps,),
        left_specs + plain,
        pl.BlockSpec((1, tokens), whole_index),
        jax.ShapeDtypeStruct((1, tokens), F32),
        [gram] * 2 + extra,
        (4 * tokens * tokens * width, 8 * tokens * width, 0),
    )(flags, *pieces, right, right_turned)
    return jnp.sum(out)


def gradient(left_turned, right, rows, scale, flags):
    height, tokens = left_turned.shape
    width = right[0].shape[1]
    n = len(right)

    def kernel(flags_ref, scale_ref, left_ref, *refs):
        out_ref = refs[n]
        if n == 1:
            right_all = refs[0][...]
        else:
            for i, ref in enumerate(refs[:n]):
                refs[n + 1][i * rows : (i + 1) * rows, :] = ref[...]
            right_all = refs[n + 1][...]
        product = lax.dot_general(
            left_ref[...], right_all, PLAIN, preferred_element_type=F32
        )
        out_ref[...] = (product * scale_ref[0, 0]).astype(BF16)

    return call(
        kernel,
        (width // TILE,),
        [
            pl.BlockSpec(memory_space=pltpu.SMEM),
            pl.BlockSpec((height, tokens), whole_index),
        ]
        + [pl.BlockSpec((piece.shape[0], TILE), column_index) for piece in right],
        pl.BlockSpec((height, TILE), column_index),
        jax.ShapeDtypeStruct((height, width), BF16),
        [pltpu.VMEM((tokens, TILE), BF16)] if n > 1 else [],
        (2 * tokens * width * height, 2 * width * height + 2 * tokens * (width + height), 0),
    )(flags, scale.reshape(1, 1), left_turned, *right)


def after(value, event):
    return lax.optimization_barrier((value, event))[0]


def on_device(inputs, pre_act, out_grad, token_valid, poison, w_up, w_down):
    n_row = lax.axis_size("row")
    n_col = lax.axis_size("col")
    rows = inputs.shape[0]
    tokens = rows * n_row
    slots = n_row // 2
    row, col = lax.axis_index("row"), lax.axis_index("col")
    core = col % 2
    flags = jnp.stack([row, core]).astype(jnp.int32)
    row_bits, col_bits = bits_of(n_row), bits_of(n_col)

    masked = {0: out_grad * token_valid.astype(BF16)[:, None]}
    for bit in reversed(row_bits):
        for index in sorted(masked):
            masked[index | bit] = swap(masked[index], "row", bit)

    pre_all = lax.all_gather(pre_act, "col", axis=0, tiled=True)
    inputs_all = lax.all_gather(after(inputs, pre_all), "row", axis=0, tiled=True)
    act, act_turned, slope = gelu_all(pre_all, flags, n_row, rows)

    groups = 2 if slots % 2 == 0 else 1
    per_group = slots // groups
    kept, sent = [], []
    for group in range(groups):
        chosen = range(group * per_group, (group + 1) * per_group)
        keep, send = act_grad_part(
            [masked[2 * slot] for slot in chosen],
            [masked[2 * slot + 1] for slot in chosen],
            w_down,
            flags,
        )
        total = keep + swap(send, "col", 1).astype(F32)
        for bit in col_bits[1:]:
            total = total + swap(total.astype(BF16), "col", bit).astype(F32)
        first = group * per_group * rows
        hidden = (total * slope[first : first + per_group * rows]).astype(BF16)
        kept.append(hidden)
        sent.append(swap(hidden, "col", 1))

    def hidden_place(half, slot):
        return lambda row, core: turned(2 * slot + (half ^ core), n_row)

    hidden_places = [
        [hidden_place(half, group * per_group + k) for k in range(per_group)]
        for half in range(2)
        for group in range(groups)
    ]
    hidden_all, hidden_turned = arrange(kept + sent, hidden_places, tokens, rows, flags)

    def inputs_place(source):
        return lambda row, core: turned(row ^ source, n_row)

    inputs_all, inputs_turned = arrange(
        [inputs_all], [[inputs_place(source) for source in range(n_row)]], tokens, rows, flags
    )
    masked_blocks = [masked[turned(place, n_row)] for place in range(n_row)]

    model = w_up.shape[0]
    parts = 3 if model % (3 * TILE) == 0 else 1
    step = model // parts
    input_sums = []
    for part in range(parts):
        total, theirs = input_part(hidden_turned, w_up, part * step, step, flags)
        total = total + swap(theirs, "row", 1).astype(F32)
        for bit in row_bits[1:]:
            half = total.shape[0] // 2
            total = total[:half] + swap(total[half:].astype(BF16), "row", bit).astype(F32)
        input_sums.append(total)

    square_term = gram_inner(
        masked_blocks, None, act, act_turned, rows, flags
    ) + gram_inner(inputs_all, inputs_turned, hidden_all, hidden_turned, rows, flags)
    flag_value = poison[0, 0].astype(F32)
    keep_block = 1.0 - flag_value
    count_term = jnp.where(col == 0, jnp.sum(token_valid.astype(F32)), 0.0)
    scalars = jnp.stack([count_term, keep_block * square_term, flag_value])
    for axis, bits in (("col", col_bits), ("row", row_bits)):
        for bit in bits:
            scalars = scalars + swap(scalars, axis, bit)
    count_all, square_all, flag_all = scalars[0], jnp.maximum(scalars[1], 0.0), scalars[2]

    token_total = jnp.maximum(count_all, 1.0)
    squares = square_all / (token_total * token_total)
    block_count = float(n_row * n_col)
    estimate = squares * block_count / jnp.maximum(block_count - flag_all, 1.0)
    model_width = w_up.shape[0] * n_col
    hidden_width = w_up.shape[1] * n_row
    limit = 0.25 * math.sqrt(hidden_width * model_width / tokens)
    clip_factor = jnp.minimum(1.0, limit / jnp.sqrt(estimate + 1e-06))
    scale = keep_block * clip_factor / token_total
    grad_down = gradient(act_turned, masked_blocks, rows, scale, flags)
    grad_up = gradient(inputs_turned, [hidden_all], rows, scale, flags)
    input_sum = jnp.concatenate(input_sums, axis=1)
    return (input_sum / token_total).astype(BF16), grad_up, grad_down


def solution(mesh):
    placed = (
        P("row", "col"),
        P("col", "row"),
        P("row", "col"),
        P("row"),
        P("row", "col"),
        P("col", "row"),
        P("row", "col"),
    )
    return jax.shard_map(
        on_device,
        mesh=mesh,
        in_specs=placed,
        out_specs=(P("row", "col"), P("col", "row"), P("row", "col")),
        check_vma=False,
    )
```

```python
import math

import jax
import jax.numpy as jnp
from jax import lax
from jax.experimental import pallas as pl
from jax.experimental.pallas import tpu as pltpu
from jax.sharding import PartitionSpec as P

F32 = jnp.float32
BF16 = jnp.bfloat16
LAST = (((1,), (1,)), ((), ()))
PLAIN = (((1,), (0,)), ((), ()))
FACTOR = math.sqrt(2.0 / math.pi)
TILE = 256
VMEM_LIMIT = 56 * 1024 * 1024


def swap(value, axis, bit):
    size = lax.axis_size(axis)
    return lax.ppermute(value, axis, [(i, i ^ bit) for i in range(size)])


def bits_of(size):
    return [1 << i for i in range(size.bit_length() - 1)]


def turned(index, size):
    return sum(((index // bit) % 2) * (size // 2 // bit) for bit in bits_of(size))


def call(kernel, grid, in_specs, out_specs, out_shape, scratch, cost, aliases=None):
    flops, moved, slow = cost
    return pl.pallas_call(
        kernel,
        grid_spec=pltpu.PrefetchScalarGridSpec(
            num_scalar_prefetch=1,
            grid=grid,
            in_specs=in_specs,
            out_specs=out_specs,
            scratch_shapes=scratch,
        ),
        out_shape=out_shape,
        input_output_aliases=aliases or {},
        compiler_params=pltpu.CompilerParams(
            dimension_semantics=("arbitrary",), vmem_limit_bytes=VMEM_LIMIT
        ),
        cost_estimate=pl.CostEstimate(
            flops=flops, bytes_accessed=moved, transcendentals=slow
        ),
    )


def whole_index(i, flags):
    return (0, 0)


def column_index(i, flags):
    return (0, i)


def aligned(start):
    return pl.multiple_of(start, 16)


def gelu_all(pre_all, flags, n_row, rows):
    tokens, width = pre_all.shape

    def kernel(flags_ref, pre_ref, act_ref, slope_ref):
        row, core = flags_ref[0], flags_ref[1]
        for source in range(n_row):
            index = row ^ source
            hval = pre_ref[source * rows : (source + 1) * rows, :].astype(F32)
            tanh_part = jnp.tanh(FACTOR * (hval + 0.044715 * hval * hval * hval))
            act_ref[pl.ds(aligned(turned(index, n_row) * rows), rows), :] = (
                0.5 * hval * (1.0 + tanh_part)
            ).astype(BF16)

            @pl.when(index % 2 == core)
            def _():
                slope_ref[pl.ds(aligned((index // 2) * rows), rows), :] = 0.5 * (
                    1.0 + tanh_part
                ) + 0.5 * hval * (1.0 - tanh_part * tanh_part) * FACTOR * (
                    1.0 + 3.0 * 0.044715 * hval * hval
                )

    return call(
        kernel,
        (width // TILE,),
        [pl.BlockSpec((tokens, TILE), column_index)],
        [
            pl.BlockSpec((tokens, TILE), column_index),
            pl.BlockSpec((tokens // 2, TILE), column_index),
        ],
        [
            jax.ShapeDtypeStruct((tokens, width), BF16),
            jax.ShapeDtypeStruct((tokens // 2, width), F32),
        ],
        [],
        (30 * tokens * width, 6 * tokens * width, tokens * width),
    )(flags, pre_all)


def arrange(chunks, places, rows, flags):
    width = chunks[0][0].shape[1]
    tokens = sum(piece.shape[0] for piece in chunks[0])
    tile = 2 * TILE if width % (2 * TILE) == 0 else TILE
    tiles = width // tile
    n = len(places)

    def kernel(flags_ref, *refs):
        row, core = flags_ref[0], flags_ref[1]

        def fill(pieces):
            for ref, blocks in zip(pieces, places):
                for k, place in enumerate(blocks):
                    refs[-1][pl.ds(aligned(place(row, core) * rows), rows), :] = ref[
                        k * rows : (k + 1) * rows, :
                    ]

        for c in range(len(chunks)):
            pl.when(pl.program_id(0) // tiles == c)(lambda c=c: fill(refs[c * n : c * n + n]))

    def of_chunk(c):
        return lambda i, flags: (0, jnp.clip(i - c * tiles, 0, tiles - 1))

    return call(
        kernel,
        (tiles * len(chunks),),
        [
            pl.BlockSpec((piece.shape[0], tile), of_chunk(c))
            for c, pieces in enumerate(chunks)
            for piece in pieces
        ],
        pl.BlockSpec((tokens, tile), column_index),
        jax.ShapeDtypeStruct((tokens, width * len(chunks)), BF16),
        [],
        (0, 4 * tokens * width * len(chunks), 0),
    )(flags, *[piece for pieces in chunks for piece in pieces])


def stack(target, refs):
    if len(refs) == 1:
        return refs[0]
    start = 0
    for ref in refs:
        target[start : start + ref.shape[0], :] = ref[...]
        start += ref.shape[0]
    return target


def gram_inner(left, right, flags):
    n, m = len(left), len(right)
    tokens = sum(piece.shape[0] for piece in left)
    width = left[0].shape[1]
    tile = 2 * TILE if width % (2 * TILE) == 0 else TILE
    steps = width // tile

    def kernel(flags_ref, *refs):
        out_ref, left_all, right_all, left_gram, right_gram = refs[n + m :]
        step = pl.program_id(0)
        left_rows = stack(left_all, refs[:n])
        right_rows = stack(right_all, refs[n : n + m])

        @pl.when(step == 0)
        def _():
            left_gram[...] = jnp.zeros_like(left_gram)
            right_gram[...] = jnp.zeros_like(right_gram)

        for rows, total in ((left_rows, left_gram), (right_rows, right_gram)):
            total[...] += lax.dot_general(
                rows[...], rows[...], LAST, preferred_element_type=F32
            )

        @pl.when(step == steps - 1)
        def _():
            out_ref[...] = jnp.sum(left_gram[...] * right_gram[...], axis=0, keepdims=True)

    gram = pltpu.VMEM((tokens, tokens), F32)
    out = call(
        kernel,
        (steps,),
        [pl.BlockSpec((piece.shape[0], tile), column_index) for piece in left + right],
        pl.BlockSpec((1, tokens), whole_index),
        jax.ShapeDtypeStruct((1, tokens), F32),
        [pltpu.VMEM((tokens, tile), BF16)] * 2 + [gram] * 2,
        (4 * tokens * tokens * width, 4 * tokens * width, 0),
    )(flags, *left, *right)
    return jnp.sum(out)


def gradient(left, right, scale, flags, part, parts, before):
    height, width = left[0].shape[1], right[0].shape[1]
    tokens = sum(piece.shape[0] for piece in left)
    tile = 2 * TILE if height % (2 * TILE * parts) == 0 else TILE
    steps = height // tile // parts
    across = next(n for n in (768, 512, 256, width) if width % n == 0)
    n, m = len(left), len(right)

    def kernel(flags_ref, scale_ref, *refs):
        out_ref, left_all, right_all = refs[-3:]

        @pl.when(pl.program_id(0) == 0)
        def _():
            stack(right_all, refs[n : n + m])

        right_rows = refs[n] if m == 1 else right_all
        left_turned = stack(left_all, refs[:n])[...].T
        for start in range(0, width, across):
            product = lax.dot_general(
                left_turned,
                right_rows[:, start : start + across],
                PLAIN,
                preferred_element_type=F32,
            )
            out_ref[:, start : start + across] = (product * scale_ref[0, 0]).astype(BF16)

    def rows_of_part(i, flags):
        return (part * steps + i, 0)

    operands = [flags, scale.reshape(1, 1), *left, *right]
    in_specs = (
        [pl.BlockSpec(memory_space=pltpu.SMEM)]
        + [
            pl.BlockSpec((piece.shape[0], tile), lambda i, flags: (0, part * steps + i))
            for piece in left
        ]
        + [pl.BlockSpec((piece.shape[0], width), whole_index) for piece in right]
    )
    aliases = {}
    if before is not None:
        aliases = {len(operands): 0}
        operands.append(before)
        in_specs.append(pl.BlockSpec(memory_space=pl.ANY))
    return call(
        kernel,
        (steps,),
        in_specs,
        pl.BlockSpec((tile, width), rows_of_part),
        jax.ShapeDtypeStruct((height, width), BF16),
        [
            pltpu.VMEM((tokens, tile) if n > 1 else (16, 128), BF16),
            pltpu.VMEM((tokens, width) if m > 1 else (16, 128), BF16),
        ],
        (
            2 * tokens * width * height // parts,
            2 * width * height // parts + 2 * tokens * (width + height),
            0,
        ),
        aliases,
    )(*operands)


def after(value, *events):
    return lax.optimization_barrier((value, *events))[0]


def on_device(inputs, pre_act, out_grad, token_valid, poison, w_up, w_down):
    n_row = lax.axis_size("row")
    n_col = lax.axis_size("col")
    rows = inputs.shape[0]
    tokens = rows * n_row
    slots = n_row // 2
    row, col = lax.axis_index("row"), lax.axis_index("col")
    core = col % 2
    flags = jnp.stack([row, core]).astype(jnp.int32)
    row_bits, col_bits = bits_of(n_row), bits_of(n_col)

    def exchange(own, first_hop):
        blocks = {0: own}
        for bit in reversed(row_bits[1:]):
            for index in sorted(blocks):
                if index % 2 == 0:
                    source = blocks[index] if index == 0 else after(blocks[index], blocks[1])
                    blocks[index | bit] = swap(source, "row", bit)
                    if 1 not in blocks:
                        blocks[1] = swap(first_hop(own), "row", 1)
        for index in sorted(blocks):
            if index % 2 == 0 and index > 0:
                blocks[index | 1] = swap(blocks[index], "row", 1)
        return [blocks[index] for index in range(n_row)]

    pre_all = lax.all_gather(pre_act, "col", axis=0, tiled=True)
    masked = exchange(out_grad * token_valid.astype(BF16)[:, None], lambda own: own)
    inputs_all = exchange(after(inputs, masked[-2]), lambda own: after(own, masked[-1]))

    def group_place(index):
        return lambda row, core: ((index % 2) ^ core) * slots + index // 2

    block = arrange(
        [masked], [[group_place(index)] for index in range(n_row)], rows, flags
    )
    block = after(block, pre_all)
    half = tokens // 2
    hidden_width = w_down.shape[0]
    parts = 3 if hidden_width % (3 * TILE) == 0 else 1
    step = hidden_width // parts
    totals = []
    for part in range(parts):
        if part == parts - 1:
            block = after(block, inputs_all[2], *totals[:-1])
        partial = lax.dot_general(
            block, w_down[part * step : (part + 1) * step], LAST, preferred_element_type=F32
        )
        other = swap(partial[half:].astype(BF16), "col", 1)
        totals.append(partial[:half] + other.astype(F32))
    act, slope = gelu_all(
        after(pre_all, inputs_all[1], inputs_all[n_row // 2]), flags, n_row, rows
    )
    masked_blocks = [masked[turned(place, n_row)] for place in range(n_row)]
    square_down = gram_inner(
        masked_blocks, [after(act, inputs_all[3], inputs_all[-2])], flags
    )
    hidden_pieces = []
    for part, total in enumerate(totals):
        for bit in col_bits[1:]:
            total = total + swap(total.astype(BF16), "col", bit).astype(F32)
        hidden = (total * slope[:, part * step : (part + 1) * step]).astype(BF16)
        hidden_pieces.append([hidden, swap(hidden, "col", 1)])

    def hidden_place(side, slot):
        return lambda row, core: turned(2 * slot + (side ^ core), n_row)

    hidden_places = [[hidden_place(side, slot) for slot in range(slots)] for side in range(2)]
    hidden_pieces[0][0] = after(hidden_pieces[0][0], square_down, *inputs_all)
    hidden_all = arrange(hidden_pieces, hidden_places, rows, flags)
    inputs_blocks = [inputs_all[turned(place, n_row)] for place in range(n_row)]

    model = w_up.shape[0]
    parts = 3 if model % (3 * TILE) == 0 else 1
    step = model // parts
    flag_value = poison[0, 0].astype(F32)
    keep_block = 1.0 - flag_value
    count_term = jnp.where(col == 0, jnp.sum(token_valid.astype(F32)), 0.0)
    stages, partials = [], []
    operand = hidden_all
    for part in range(parts):
        partial = lax.dot_general(
            operand, w_up[part * step : (part + 1) * step], LAST, preferred_element_type=F32
        )
        partials.append(partial)
        theirs = partial[half:].astype(BF16)
        total = partial[:half] + swap(theirs, "row", 1).astype(F32)
        stages.append([total])
        for bit in row_bits[1:]:
            split = total.shape[0] // 2
            total = total[:split] + swap(total[split:].astype(BF16), "row", bit).astype(F32)
            stages[-1].append(total)
        if part == 0:
            square_up = gram_inner(inputs_blocks, [after(hidden_all, theirs)], flags)
            scalars = jnp.stack(
                [count_term, keep_block * (square_down + square_up), flag_value]
            )
            for bit in col_bits:
                scalars = scalars + swap(scalars, "col", bit)
            operand = after(hidden_all, scalars, stages[0][0])
        else:
            operand = after(operand, stages[0][1])
    for hop, bit in enumerate(row_bits):
        if 0 < hop < parts:
            scalars = after(scalars, partials[hop])
        scalars = scalars + swap(scalars, "row", bit)
    count_all, square_all, flag_all = scalars[0], jnp.maximum(scalars[1], 0.0), scalars[2]

    token_total = jnp.maximum(count_all, 1.0)
    squares = square_all / (token_total * token_total)
    block_count = float(n_row * n_col)
    estimate = squares * block_count / jnp.maximum(block_count - flag_all, 1.0)
    limit = 0.25 * math.sqrt(
        (w_up.shape[1] * n_row) * (w_up.shape[0] * n_col) / tokens
    )
    clip_factor = jnp.minimum(1.0, limit / jnp.sqrt(estimate + 1e-06))
    scale = keep_block * clip_factor / token_total

    grads = []
    call_index = 0
    for left, right in (([act], masked_blocks), (inputs_blocks, [hidden_all])):
        out = None
        for part in range(2):
            events = [
                stage[call_index - i + 1]
                for i, stage in enumerate(stages)
                if 0 <= call_index - i + 1 < len(stage)
            ]
            out = gradient(left, right, after(scale, *events), flags, part, 2, out)
            call_index += 1
        grads.append(out)
    input_sum = jnp.concatenate([stage[-1] for stage in stages], axis=1)
    return (input_sum / token_total).astype(BF16), grads[1], grads[0]


def solution(mesh):
    placed = (
        P("row", "col"),
        P("col", "row"),
        P("row", "col"),
        P("row"),
        P("row", "col"),
        P("col", "row"),
        P("row", "col"),
    )
    return jax.shard_map(
        on_device,
        mesh=mesh,
        in_specs=placed,
        out_specs=(P("row", "col"), P("col", "row"), P("row", "col")),
        check_vma=False,
    )
```

```python
import math

import jax
import jax.numpy as jnp
from jax import lax
from jax.experimental import pallas as pl
from jax.experimental.pallas import tpu as pltpu
from jax.sharding import PartitionSpec as P

F32 = jnp.float32
BF16 = jnp.bfloat16
LAST = (((1,), (1,)), ((), ()))
FIRST = (((0,), (0,)), ((), ()))
FACTOR = math.sqrt(2.0 / math.pi)
TILE = 256
VMEM_LIMIT = 56 * 1024 * 1024


def swap(value, axis, bit):
    size = lax.axis_size(axis)
    return lax.ppermute(value, axis, [(i, i ^ bit) for i in range(size)])


def bits_of(size):
    return [1 << i for i in range(size.bit_length() - 1)]


def turned(index, size):
    return sum(((index // bit) % 2) * (size // 2 // bit) for bit in bits_of(size))


def call(kernel, grid, in_specs, out_specs, out_shape, scratch, cost, aliases=None):
    flops, moved, slow = cost
    return pl.pallas_call(
        kernel,
        grid_spec=pltpu.PrefetchScalarGridSpec(
            num_scalar_prefetch=1,
            grid=grid,
            in_specs=in_specs,
            out_specs=out_specs,
            scratch_shapes=scratch,
        ),
        out_shape=out_shape,
        input_output_aliases=aliases or {},
        compiler_params=pltpu.CompilerParams(
            dimension_semantics=("arbitrary",), vmem_limit_bytes=VMEM_LIMIT
        ),
        cost_estimate=pl.CostEstimate(
            flops=flops, bytes_accessed=moved, transcendentals=slow
        ),
    )


def whole_index(i, flags):
    return (0, 0)


def column_index(i, flags):
    return (0, i)


def aligned(start):
    return pl.multiple_of(start, 16)


def token_place(side, order, core, per_group):
    group, k = order // per_group, order % per_group
    return (2 * group + (side ^ core)) * per_group + k


def gelu_all(pre_all, flags, n_row, per_group, rows):
    tokens, width = pre_all.shape
    slots = n_row // 2

    def kernel(flags_ref, pre_ref, act_ref, slope_ref):
        row, core = flags_ref[0], flags_ref[1]
        for source in range(n_row):
            index = row ^ source
            hval = pre_ref[source * rows : (source + 1) * rows, :].astype(F32)
            tanh_part = jnp.tanh(FACTOR * (hval + 0.044715 * hval * hval * hval))
            order = turned(index // 2, slots)
            place = token_place(index % 2, order, core, per_group)
            act_ref[pl.ds(aligned(place * rows), rows), :] = (
                0.5 * hval * (1.0 + tanh_part)
            ).astype(BF16)

            @pl.when(index % 2 == core)
            def _():
                slope_ref[pl.ds(aligned(order * rows), rows), :] = 0.5 * (
                    1.0 + tanh_part
                ) + 0.5 * hval * (1.0 - tanh_part * tanh_part) * FACTOR * (
                    1.0 + 3.0 * 0.044715 * hval * hval
                )

    return call(
        kernel,
        (width // TILE,),
        [pl.BlockSpec((tokens, TILE), column_index)],
        [
            pl.BlockSpec((tokens, TILE), column_index),
            pl.BlockSpec((tokens // 2, TILE), column_index),
        ],
        [
            jax.ShapeDtypeStruct((tokens, width), BF16),
            jax.ShapeDtypeStruct((tokens // 2, width), F32),
        ],
        [],
        (30 * tokens * width, 6 * tokens * width, tokens * width),
    )(flags, pre_all)


def arrange(pieces, places, rows, flags):
    width = pieces[0].shape[1]
    tokens = sum(piece.shape[0] for piece in pieces)
    tile = 2 * TILE if width % (2 * TILE) == 0 else TILE

    def kernel(flags_ref, *refs):
        for ref, place in zip(refs, places):
            refs[-1][pl.ds(aligned(place(flags_ref[1]) * rows), rows), :] = ref[...]

    return call(
        kernel,
        (width // tile,),
        [pl.BlockSpec((rows, tile), column_index)] * len(pieces),
        pl.BlockSpec((tokens, tile), column_index),
        jax.ShapeDtypeStruct((tokens, width), BF16),
        [],
        (0, 4 * tokens * width, 0),
    )(flags, *pieces)


def gram_inner(left, right, flags):
    tokens, width = left.shape
    tile = 2 * TILE if width % (2 * TILE) == 0 else TILE
    steps = width // tile

    def kernel(flags_ref, left_ref, right_ref, out_ref, left_gram, right_gram):
        step = pl.program_id(0)

        @pl.when(step == 0)
        def _():
            left_gram[...] = jnp.zeros_like(left_gram)
            right_gram[...] = jnp.zeros_like(right_gram)

        for ref, total in ((left_ref, left_gram), (right_ref, right_gram)):
            total[...] += lax.dot_general(
                ref[...], ref[...], LAST, preferred_element_type=F32
            )

        @pl.when(step == steps - 1)
        def _():
            out_ref[...] = jnp.sum(left_gram[...] * right_gram[...], axis=0, keepdims=True)

    out = call(
        kernel,
        (steps,),
        [pl.BlockSpec((tokens, tile), column_index)] * 2,
        pl.BlockSpec((1, tokens), whole_index),
        jax.ShapeDtypeStruct((1, tokens), F32),
        [pltpu.VMEM((tokens, tokens), F32)] * 2,
        (4 * tokens * tokens * width, 4 * tokens * width, 0),
    )(flags, left, right)
    return jnp.sum(out)


def after(value, *events):
    return lax.optimization_barrier((value, *events))[0]


def on_device(inputs, pre_act, out_grad, token_valid, poison, w_up, w_down):
    n_row = lax.axis_size("row")
    n_col = lax.axis_size("col")
    rows = inputs.shape[0]
    tokens = rows * n_row
    slots = n_row // 2
    row, col = lax.axis_index("row"), lax.axis_index("col")
    core = col % 2
    flags = jnp.stack([row, core]).astype(jnp.int32)
    row_bits, col_bits = bits_of(n_row), bits_of(n_col)

    def exchange(own, x_own):
        blocks = {0: own, 1: swap(x_own, "row", 1)}
        for bit in reversed(row_bits[1:]):
            for index in sorted(blocks):
                if index % 2 == 0:
                    source = own if index == 0 else after(blocks[index], blocks[1], blocks[bit])
                    blocks[index | bit] = swap(source, "row", bit)
        even = [index for index in sorted(blocks) if index % 2 == 0 and index > 0]
        for index in even:
            if not index & 2:
                blocks[index | 1] = swap(blocks[index], "row", 1)
        last = max(index for index in blocks if index & 1)
        for index in even:
            if index & 2:
                blocks[index | 1] = swap(after(blocks[index], blocks[last]), "row", 1)
        return [blocks[index] for index in range(n_row)]

    groups = 2 if slots % 2 == 0 else 1
    per_group = slots // groups
    count = per_group * rows
    by_group = [[] for _ in range(groups)]
    for index in range(n_row):
        by_group[turned(index // 2, slots) // per_group].append(index)

    def place_of(index, group):
        order = turned(index // 2, slots)
        return lambda core: token_place(index % 2, order, core, per_group) - (
            group * 2 * per_group
        )

    pre_all = lax.all_gather(pre_act, "col", axis=0, tiled=True)
    own = out_grad * token_valid.astype(BF16)[:, None]
    masked = exchange(own, own)
    own = after(inputs, masked[-2])
    inputs_blocks = exchange(own, after(own, masked[-1]))

    blocks, totals = [], []
    for group, indices in enumerate(by_group):
        block = arrange(
            [masked[index] for index in indices],
            [place_of(index, group) for index in indices],
            rows,
            flags,
        )
        blocks.append(block)
        block = after(block, masked[-2], pre_all, *totals)
        partial = lax.dot_general(block, w_down, LAST, preferred_element_type=F32)
        send = partial[count:].astype(BF16)
        if group == 0:
            send = after(send, *[masked[index] for index in by_group[-1] if index & 1])
        other = swap(send, "col", 1)
        totals.append(partial[:count] + other.astype(F32))
    act, slope = gelu_all(
        after(pre_all, *totals, inputs_blocks[1], inputs_blocks[2], inputs_blocks[n_row // 2]),
        flags,
        n_row,
        per_group,
        rows,
    )
    masked_all = jnp.concatenate(blocks, axis=0)
    square_down = gram_inner(
        masked_all, after(act, inputs_blocks[n_row // 2 + 1], inputs_blocks[-2]), flags
    )
    inputs_all = arrange(
        [after(inputs_blocks[0], square_down)] + inputs_blocks[1:],
        [place_of(index, 0) for index in range(n_row)],
        rows,
        flags,
    )
    hidden_blocks = []
    for group, total in enumerate(totals):
        for bit in col_bits[1:]:
            total = total + swap(total.astype(BF16), "col", bit).astype(F32)
        hidden = (total * slope[group * count : (group + 1) * count]).astype(BF16)
        hidden_blocks += [hidden, swap(hidden, "col", 1)]
    hidden_blocks[-1] = after(hidden_blocks[-1], inputs_all)
    hidden_all = jnp.concatenate(hidden_blocks, axis=0)

    square_up = gram_inner(inputs_all, hidden_all, flags)
    flag_value = poison[0, 0].astype(F32)
    keep_block = 1.0 - flag_value
    count_term = jnp.where(col == 0, jnp.sum(token_valid.astype(F32)), 0.0)
    scalars = jnp.stack([count_term, keep_block * (square_down + square_up), flag_value])
    hops = [("col", bit) for bit in col_bits] + [("row", bit) for bit in row_bits]

    def sides(product):
        split = product.reshape(groups, 2, count, product.shape[1])
        return [
            lax.dynamic_index_in_dim(split, side, 1, keepdims=False).reshape(
                groups * count, product.shape[1]
            )
            for side in (core, 1 - core)
        ]

    model = w_up.shape[0]
    parts = 3 if model % (3 * TILE) == 0 else 1
    step = model // parts
    stages = []
    operand = after(hidden_all, square_up)
    for part in range(parts):
        product = lax.dot_general(
            operand, w_up[part * step : (part + 1) * step], LAST, preferred_element_type=F32
        )
        mine, theirs = sides(product)
        total = mine + swap(theirs.astype(BF16), "row", 1).astype(F32)
        stages.append([total])
        for bit in row_bits[1:]:
            split = total.shape[0] // 2
            total = total[:split] + swap(total[split:].astype(BF16), "row", bit).astype(F32)
            stages[-1].append(total)
        axis, bit = hops.pop(0)
        scalars = scalars + swap(scalars, axis, bit)
        operand = after(operand, scalars)
        scalars = after(scalars, product)
    for axis, bit in hops:
        scalars = scalars + swap(scalars, axis, bit)
    count_all, square_all, flag_all = scalars[0], jnp.maximum(scalars[1], 0.0), scalars[2]

    token_total = jnp.maximum(count_all, 1.0)
    squares = square_all / (token_total * token_total)
    block_count = float(n_row * n_col)
    estimate = squares * block_count / jnp.maximum(block_count - flag_all, 1.0)
    limit = 0.25 * math.sqrt(
        (w_up.shape[1] * n_row) * (w_up.shape[0] * n_col) / tokens
    )
    clip_factor = jnp.minimum(1.0, limit / jnp.sqrt(estimate + 1e-06))
    scale = keep_block * clip_factor / token_total

    def gradient(left, right, scale):
        product = lax.dot_general(left, right, FIRST, preferred_element_type=F32)
        return (product * scale).astype(BF16)

    grad_down = gradient(act, masked_all, after(scale, stages[0][0]))
    events = [stage[0] for stage in stages] + [stages[0][1], grad_down]
    grad_up = gradient(inputs_all, hidden_all, after(scale, *events))
    input_sum = jnp.concatenate([stage[-1] for stage in stages], axis=1)
    return (input_sum / token_total).astype(BF16), grad_up, grad_down


def solution(mesh):
    placed = (
        P("row", "col"),
        P("col", "row"),
        P("row", "col"),
        P("row"),
        P("row", "col"),
        P("col", "row"),
        P("row", "col"),
    )
    return jax.shard_map(
        on_device,
        mesh=mesh,
        in_specs=placed,
        out_specs=(P("row", "col"), P("col", "row"), P("row", "col")),
        check_vma=False,
    )
```

```python
import math

import jax
import jax.numpy as jnp
from jax import lax
from jax.experimental import pallas as pl
from jax.experimental.pallas import tpu as pltpu
from jax.sharding import PartitionSpec as P

F32 = jnp.float32
BF16 = jnp.bfloat16
LAST = (((1,), (1,)), ((), ()))
FIRST = (((0,), (0,)), ((), ()))
FACTOR = math.sqrt(2.0 / math.pi)
TILE = 256
VMEM_LIMIT = 56 * 1024 * 1024


def swap(value, axis, bit):
    size = lax.axis_size(axis)
    return lax.ppermute(value, axis, [(i, i ^ bit) for i in range(size)])


def bits_of(size):
    return [1 << i for i in range(size.bit_length() - 1)]


def turned(index, size):
    return sum(((index // bit) % 2) * (size // 2 // bit) for bit in bits_of(size))


def call(kernel, grid, in_specs, out_specs, out_shape, scratch, moved=1000):
    return pl.pallas_call(
        kernel,
        grid_spec=pltpu.PrefetchScalarGridSpec(
            num_scalar_prefetch=1,
            grid=grid,
            in_specs=in_specs,
            out_specs=out_specs,
            scratch_shapes=scratch,
        ),
        out_shape=out_shape,
        compiler_params=pltpu.CompilerParams(
            dimension_semantics=("arbitrary",), vmem_limit_bytes=VMEM_LIMIT
        ),
        cost_estimate=pl.CostEstimate(
            flops=1000, bytes_accessed=moved, transcendentals=0
        ),
    )


def whole_index(i, flags):
    return (0, 0)


def column_index(i, flags):
    return (0, i)


def aligned(start):
    return pl.multiple_of(start, 16)


def token_place(side, order, core, per_group):
    group, k = order // per_group, order % per_group
    return (2 * group + (side ^ core)) * per_group + k


def widest(width, limit):
    return max(tile for tile in range(128, limit + 1, 128) if width % tile == 0)


def gelu_all(pieces, offsets, flags, n_row, per_group, rows):
    width = pieces[0].shape[1]
    per_col = pieces[0].shape[0] // rows
    slots = n_row // 2
    tokens = n_row * rows
    tile = widest(width, 256)

    def kernel(flags_ref, *refs):
        act_ref, slope_ref = refs[-2:]
        row, core, col = flags_ref[0], flags_ref[1], flags_ref[2]
        for ref, offset in zip(refs[:-2], offsets):
            for part in range(per_col):
                index = row ^ ((col ^ offset) * per_col + part)
                hval = ref[part * rows : (part + 1) * rows, :].astype(F32)
                tanh_part = jnp.tanh(FACTOR * (hval + 0.044715 * hval * hval * hval))
                order = turned(index // 2, slots)
                place = token_place(index % 2, order, core, per_group)
                act_ref[pl.ds(aligned(place * rows), rows), :] = (
                    0.5 * hval * (1.0 + tanh_part)
                ).astype(BF16)

                @pl.when(index % 2 == core)
                def _():
                    slope_ref[pl.ds(aligned(order * rows), rows), :] = 0.5 * (
                        1.0 + tanh_part
                    ) + 0.5 * hval * (1.0 - tanh_part * tanh_part) * FACTOR * (
                        1.0 + 3.0 * 0.044715 * hval * hval
                    )

    return call(
        kernel,
        (width // tile,),
        [pl.BlockSpec((piece.shape[0], tile), column_index) for piece in pieces],
        [
            pl.BlockSpec((tokens, tile), column_index),
            pl.BlockSpec((tokens // 2, tile), column_index),
        ],
        [
            jax.ShapeDtypeStruct((tokens, width), BF16),
            jax.ShapeDtypeStruct((tokens // 2, width), F32),
        ],
        [],
        16 * tokens * width,
    )(flags, *pieces)


def arrange(pieces, places, flags):
    rows, width = pieces[0].shape
    tokens = rows * len(pieces)
    tile = widest(width, width // 2)

    def kernel(flags_ref, *refs):
        for ref, place in zip(refs, places):
            refs[-1][pl.ds(aligned(place(flags_ref[1]) * rows), rows), :] = ref[...]

    return call(
        kernel,
        (width // tile,),
        [pl.BlockSpec((rows, tile), column_index)] * len(pieces),
        pl.BlockSpec((tokens, tile), column_index),
        jax.ShapeDtypeStruct((tokens, width), BF16),
        [],
    )(flags, *pieces)


def stack(pieces, flags):
    return arrange(pieces, [lambda core, i=i: i for i in range(len(pieces))], flags)


def gram(value, flags):
    tokens, width = value.shape
    tile = widest(width, 1024)

    def kernel(flags_ref, value_ref, out_ref):
        @pl.when(pl.program_id(0) == 0)
        def _():
            out_ref[...] = jnp.zeros_like(out_ref)

        out_ref[...] += lax.dot_general(
            value_ref[...], value_ref[...], LAST, preferred_element_type=F32
        )

    return call(
        kernel,
        (width // tile,),
        [pl.BlockSpec((tokens, tile), column_index)],
        pl.BlockSpec((tokens, tokens), whole_index),
        jax.ShapeDtypeStruct((tokens, tokens), F32),
        [],
    )(flags, value)


def gram_inner(left_gram, right, flags):
    tokens, width = right.shape
    tile = widest(width, 1024)
    steps = width // tile

    def kernel(flags_ref, left_ref, right_ref, out_ref, right_gram):
        step = pl.program_id(0)

        @pl.when(step == 0)
        def _():
            right_gram[...] = jnp.zeros_like(right_gram)

        right_gram[...] += lax.dot_general(
            right_ref[...], right_ref[...], LAST, preferred_element_type=F32
        )

        @pl.when(step == steps - 1)
        def _():
            out_ref[...] = jnp.sum(left_ref[...] * right_gram[...], axis=0, keepdims=True)

    out = call(
        kernel,
        (steps,),
        [
            pl.BlockSpec((tokens, tokens), whole_index),
            pl.BlockSpec((tokens, tile), column_index),
        ],
        pl.BlockSpec((1, tokens), whole_index),
        jax.ShapeDtypeStruct((1, tokens), F32),
        [pltpu.VMEM((tokens, tokens), F32)],
    )(flags, left_gram, right)
    return jnp.sum(out)


def after(value, *events):
    return lax.optimization_barrier((value, *events))[0]


def on_device(inputs, pre_act, out_grad, token_valid, poison, w_up, w_down):
    n_row = lax.axis_size("row")
    n_col = lax.axis_size("col")
    rows = inputs.shape[0]
    tokens = rows * n_row
    slots = n_row // 2
    row, col = lax.axis_index("row"), lax.axis_index("col")
    core = col % 2
    flags = jnp.stack([row, core, col]).astype(jnp.int32)
    row_bits, col_bits = bits_of(n_row), bits_of(n_col)

    def exchange(own, x_own, early, late):
        blocks = {0: own, 1: swap(x_own, "row", 1)}
        for bit in reversed(row_bits[1:]):
            for index in sorted(blocks):
                if index % 2 == 0:
                    source = own if index == 0 else after(blocks[index], blocks[1], blocks[bit])
                    blocks[index | bit] = swap(source, "row", bit)
        even = [index for index in sorted(blocks) if index % 2 == 0 and index > 0]
        for index in even:
            if not index & 2:
                blocks[index | 1] = swap(after(blocks[index], early), "row", 1)
        last = max(index for index in blocks if index & 1)
        for index in even:
            if index & 2:
                blocks[index | 1] = swap(after(blocks[index], blocks[last], late), "row", 1)
        return [blocks[index] for index in range(n_row)]

    groups = 2 if slots % 2 == 0 else 1
    per_group = slots // groups
    count = per_group * rows
    by_group = [[] for _ in range(groups)]
    for index in range(n_row):
        by_group[turned(index // 2, slots) // per_group].append(index)

    def place_of(index, group):
        order = turned(index // 2, slots)
        return lambda core: token_place(index % 2, order, core, per_group) - (
            group * 2 * per_group
        )

    pieces, offsets = [pre_act], [0]
    for bit in reversed(col_bits):
        pieces = pieces + [swap(piece, "col", bit) for piece in pieces]
        offsets = offsets + [offset ^ bit for offset in offsets]

    own = out_grad * token_valid.astype(BF16)[:, None]
    act, slope = gelu_all(pieces, offsets, flags, n_row, per_group, rows)
    masked = exchange(own, own, pieces[1], act)
    own = after(inputs, masked[-2])
    inputs_blocks = exchange(own, after(own, masked[-1]), own, own)

    blocks, totals = [], []
    for group, indices in enumerate(by_group):
        block = arrange(
            [masked[index] for index in indices],
            [place_of(index, group) for index in indices],
            flags,
        )
        blocks.append(block)
        if group == 0:
            first = [masked[-2], act]
            second = [masked[index] for index in by_group[-1] if index & 1]
        else:
            first = totals
            second = [inputs_blocks[2], inputs_blocks[n_row // 2]]
        partial = lax.dot_general(
            after(block, *first), w_down, LAST, preferred_element_type=F32
        )
        other = swap(after(partial[count:].astype(BF16), *second), "col", 1)
        totals.append(partial[:count] + other.astype(F32))
    masked_all = stack(blocks, flags)
    square_down = gram_inner(
        gram(masked_all, flags),
        after(act, *inputs_blocks[1::2][: slots // 2], inputs_blocks[-2]),
        flags,
    )
    inputs_all = arrange(
        [after(inputs_blocks[0], square_down)] + inputs_blocks[1:],
        [place_of(index, 0) for index in range(n_row)],
        flags,
    )
    inputs_gram = gram(inputs_all, flags)
    hidden_blocks = []
    for group, total in enumerate(totals):
        for bit in col_bits[1:]:
            got = swap(total.astype(BF16), "col", bit)
            if hidden_blocks:
                got = after(got, hidden_blocks[-1], square_down)
            total = total + got.astype(F32)
        hidden = (total * slope[group * count : (group + 1) * count]).astype(BF16)
        hidden_blocks += [hidden, swap(hidden, "col", 1)]
    hidden_blocks[-1] = after(hidden_blocks[-1], inputs_gram)
    hidden_all = stack(hidden_blocks, flags)

    flag_value = poison[0, 0].astype(F32)
    keep_block = 1.0 - flag_value
    count_term = jnp.where(col == 0, jnp.sum(token_valid.astype(F32)), 0.0)

    def sides(product):
        split = product.reshape(groups, 2, count, product.shape[1])
        return [
            lax.dynamic_index_in_dim(split, side, 1, keepdims=False).reshape(
                groups * count, product.shape[1]
            )
            for side in (core, 1 - core)
        ]

    model = w_up.shape[0]
    parts = 3 if model % (3 * TILE) == 0 else 1
    step = model // parts
    stages = []
    operand = hidden_all
    for part in range(parts):
        product = lax.dot_general(
            operand, w_up[part * step : (part + 1) * step], LAST, preferred_element_type=F32
        )
        mine, theirs = sides(product)
        theirs = theirs.astype(BF16)
        total = mine + swap(theirs, "row", 1).astype(F32)
        stages.append([total])
        for bit in row_bits[1:]:
            split = total.shape[0] // 2
            total = total[:split] + swap(total[split:].astype(BF16), "row", bit).astype(F32)
            stages[-1].append(total)
        if part == 0:
            square_up = gram_inner(inputs_gram, after(hidden_all, theirs), flags)
        operand = after(operand, square_up, theirs)
    scalars = jnp.stack([count_term, keep_block * (square_down + square_up), flag_value])
    scalars = after(scalars, product)
    for axis, bits in (("col", col_bits), ("row", row_bits)):
        for bit in bits:
            scalars = scalars + swap(scalars, axis, bit)
    count_all, square_all, flag_all = scalars[0], jnp.maximum(scalars[1], 0.0), scalars[2]

    token_total = jnp.maximum(count_all, 1.0)
    squares = square_all / (token_total * token_total)
    block_count = float(n_row * n_col)
    estimate = squares * block_count / jnp.maximum(block_count - flag_all, 1.0)
    limit = 0.25 * math.sqrt(
        (w_up.shape[1] * n_row) * (w_up.shape[0] * n_col) / tokens
    )
    clip_factor = jnp.minimum(1.0, limit / jnp.sqrt(estimate + 1e-06))
    scale = keep_block * clip_factor / token_total

    def gradient(left, right, scale):
        product = lax.dot_general(left, right, FIRST, preferred_element_type=F32)
        return (product * scale).astype(BF16)

    grad_down = gradient(act, masked_all, after(scale, *[stage[0] for stage in stages]))
    events = [stage[1] for stage in stages] + [grad_down]
    grad_up = gradient(inputs_all, hidden_all, after(scale, *events))
    input_sum = jnp.concatenate([stage[-1] for stage in stages], axis=1)
    return (input_sum / token_total).astype(BF16), grad_up, grad_down


def solution(mesh):
    placed = (
        P("row", "col"),
        P("col", "row"),
        P("row", "col"),
        P("row"),
        P("row", "col"),
        P("col", "row"),
        P("row", "col"),
    )
    return jax.shard_map(
        on_device,
        mesh=mesh,
        in_specs=placed,
        out_specs=(P("row", "col"), P("col", "row"), P("row", "col")),
        check_vma=False,
    )
```

```python
import math

import jax
import jax.numpy as jnp
from jax import lax
from jax.experimental import pallas as pl
from jax.experimental.pallas import tpu as pltpu
from jax.sharding import PartitionSpec as P

F32 = jnp.float32
BF16 = jnp.bfloat16
LAST = (((1,), (1,)), ((), ()))
FIRST = (((0,), (0,)), ((), ()))
FACTOR = math.sqrt(2.0 / math.pi)
TILE = 256
VMEM_LIMIT = 56 * 1024 * 1024


def swap(value, axis, bit):
    size = lax.axis_size(axis)
    return lax.ppermute(value, axis, [(i, i ^ bit) for i in range(size)])


def bits_of(size):
    return [1 << i for i in range(size.bit_length() - 1)]


def turned(index, size):
    return sum(((index // bit) % 2) * (size // 2 // bit) for bit in bits_of(size))


def call(kernel, grid, in_specs, out_specs, out_shape, moved):
    return pl.pallas_call(
        kernel,
        grid_spec=pltpu.PrefetchScalarGridSpec(
            num_scalar_prefetch=1,
            grid=grid,
            in_specs=in_specs,
            out_specs=out_specs,
        ),
        out_shape=out_shape,
        compiler_params=pltpu.CompilerParams(
            dimension_semantics=("arbitrary",), vmem_limit_bytes=VMEM_LIMIT
        ),
        cost_estimate=pl.CostEstimate(
            flops=1000, bytes_accessed=moved, transcendentals=0
        ),
    )


def whole_index(i, flags):
    return (0, 0)


def column_index(i, flags):
    return (0, i)


def aligned(start):
    return pl.multiple_of(start, 16)


def token_place(side, order, core, per_group):
    group, k = order // per_group, order % per_group
    return (2 * group + (side ^ core)) * per_group + k


def widest(width, limit):
    return max(tile for tile in range(128, limit + 1, 128) if width % tile == 0)


def gelu_all(pieces, offsets, flags, n_row, per_group, rows):
    width = pieces[0].shape[1]
    per_col = pieces[0].shape[0] // rows
    slots = n_row // 2
    tokens = n_row * rows
    tile = widest(width, 256)

    def kernel(flags_ref, *refs):
        act_ref, slope_ref = refs[-2:]
        row, core, col = flags_ref[0], flags_ref[1], flags_ref[2]
        for ref, offset in zip(refs[:-2], offsets):
            for part in range(per_col):
                index = row ^ ((col ^ offset) * per_col + part)
                hval = ref[part * rows : (part + 1) * rows, :].astype(F32)
                tanh_part = jnp.tanh(FACTOR * (hval + 0.044715 * hval * hval * hval))
                order = turned(index // 2, slots)
                place = token_place(index % 2, order, core, per_group)
                act_ref[pl.ds(aligned(place * rows), rows), :] = (
                    0.5 * hval * (1.0 + tanh_part)
                ).astype(BF16)

                @pl.when(index % 2 == core)
                def _():
                    slope_ref[pl.ds(aligned(order * rows), rows), :] = 0.5 * (
                        1.0 + tanh_part
                    ) + 0.5 * hval * (1.0 - tanh_part * tanh_part) * FACTOR * (
                        1.0 + 3.0 * 0.044715 * hval * hval
                    )

    return call(
        kernel,
        (width // tile,),
        [pl.BlockSpec((piece.shape[0], tile), column_index) for piece in pieces],
        [
            pl.BlockSpec((tokens, tile), column_index),
            pl.BlockSpec((tokens // 2, tile), column_index),
        ],
        [
            jax.ShapeDtypeStruct((tokens, width), BF16),
            jax.ShapeDtypeStruct((tokens // 2, width), F32),
        ],
        1000,
    )(flags, *pieces)


def arrange(pieces, places, flags):
    rows, width = pieces[0].shape
    tokens = rows * len(pieces)
    tile = widest(width, width // 2)

    def kernel(flags_ref, *refs):
        for ref, place in zip(refs, places):
            refs[-1][pl.ds(aligned(place(flags_ref[1]) * rows), rows), :] = ref[...]

    return call(
        kernel,
        (width // tile,),
        [pl.BlockSpec((rows, tile), column_index)] * len(pieces),
        pl.BlockSpec((tokens, tile), column_index),
        jax.ShapeDtypeStruct((tokens, width), BF16),
        6 * tokens * width,
    )(flags, *pieces)


def stack(pieces, flags):
    return arrange(pieces, [lambda core, i=i: i for i in range(len(pieces))], flags)


def gram(value):
    return lax.dot_general(value, value, LAST, preferred_element_type=F32)


def after(value, *events):
    return lax.optimization_barrier((value, *events))[0]


def on_device(inputs, pre_act, out_grad, token_valid, poison, w_up, w_down):
    n_row = lax.axis_size("row")
    n_col = lax.axis_size("col")
    rows = inputs.shape[0]
    tokens = rows * n_row
    slots = n_row // 2
    row, col = lax.axis_index("row"), lax.axis_index("col")
    core = col % 2
    flags = jnp.stack([row, core, col]).astype(jnp.int32)
    row_bits, col_bits = bits_of(n_row), bits_of(n_col)

    def first_hops(own, x_own):
        blocks = {0: own}
        for bit in reversed(row_bits):
            blocks[bit] = swap(x_own if bit == 1 else own, "row", bit)
        return blocks

    def other_hops(blocks, hop_events, x_events):
        for bit in reversed(row_bits[1:]):
            for index in sorted(blocks):
                if index > 0 and index % (2 * bit) == 0:
                    source = after(blocks[index], *hop_events)
                    blocks[index | bit] = swap(source, "row", bit)
        even = [index for index in sorted(blocks) if index % 2 == 0 and index > 0]
        for index in even:
            if not index & 2:
                blocks[index | 1] = swap(after(blocks[index], *x_events), "row", 1)
        last = max(index for index in blocks if index & 1)
        for index in even:
            if index & 2:
                blocks[index | 1] = swap(after(blocks[index], blocks[last]), "row", 1)
        return [blocks[index] for index in range(n_row)]

    groups = 2 if slots % 2 == 0 else 1
    per_group = slots // groups
    count = per_group * rows
    by_group = [[] for _ in range(groups)]
    for index in range(n_row):
        by_group[turned(index // 2, slots) // per_group].append(index)

    def place_of(index, group):
        order = turned(index // 2, slots)
        return lambda core: token_place(index % 2, order, core, per_group) - (
            group * 2 * per_group
        )

    pieces, offsets = [pre_act], [0]
    for bit in reversed(col_bits):
        pieces = pieces + [swap(piece, "col", bit) for piece in pieces]
        offsets = offsets + [offset ^ bit for offset in offsets]

    own = out_grad * token_valid.astype(BF16)[:, None]
    hops = first_hops(own, own)
    masked = other_hops(hops, [hops[bit] for bit in row_bits], [pieces[1]])
    own = after(inputs, masked[-2])
    inputs_hops = first_hops(own, after(own, masked[-1]))

    blocks, totals, received = [], [], []
    for group, indices in enumerate(by_group):
        block = arrange(
            [masked[index] for index in indices],
            [place_of(index, group) for index in indices],
            flags,
        )
        blocks.append(block)
        if group == 0:
            first = [masked[-2]]
            second = [masked[index] for index in by_group[-1] if index & 1]
        else:
            first = totals
            second = received + [inputs_hops[bit] for bit in row_bits]
        partial = lax.dot_general(
            after(block, *first), w_down, LAST, preferred_element_type=F32
        )
        total = partial[:count]
        got = swap(after(partial[count:].astype(BF16), *second), "col", 1)
        for bit in col_bits[1:]:
            total = total + got.astype(F32)
            got = swap(total.astype(BF16), "col", bit)
        totals.append(total)
        received.append(got)
    act, slope = gelu_all(
        [after(pieces[0], *totals)] + pieces[1:], offsets, flags, n_row, per_group, rows
    )
    inputs_blocks = other_hops(inputs_hops, totals[-1:], totals[-1:])
    masked_all = stack(blocks, flags)
    masked_gram = gram(after(masked_all, inputs_blocks[-2], inputs_blocks[n_row // 2 + 1]))
    square_down = jnp.sum(
        masked_gram * gram(after(act, masked_gram))
    )
    inputs_all = arrange(
        [after(inputs_blocks[0], square_down)] + inputs_blocks[1:],
        [place_of(index, 0) for index in range(n_row)],
        flags,
    )
    inputs_gram = gram(inputs_all)
    hidden_blocks = []
    for group, (total, got) in enumerate(zip(totals, received)):
        if hidden_blocks:
            got = after(got, hidden_blocks[-1], square_down)
        total = total + got.astype(F32)
        hidden = (total * slope[group * count : (group + 1) * count]).astype(BF16)
        hidden_blocks += [hidden, swap(hidden, "col", 1)]
    hidden_blocks[-1] = after(hidden_blocks[-1], inputs_gram)
    hidden_all = stack(hidden_blocks, flags)

    flag_value = poison[0, 0].astype(F32)
    keep_block = 1.0 - flag_value
    count_term = jnp.where(col == 0, jnp.sum(token_valid.astype(F32)), 0.0)

    def sides(product):
        split = product.reshape(groups, 2, count, product.shape[1])
        return [
            lax.dynamic_index_in_dim(split, side, 1, keepdims=False).reshape(
                groups * count, product.shape[1]
            )
            for side in (core, 1 - core)
        ]

    square_up = jnp.sum(inputs_gram * gram(hidden_all))
    scalars = jnp.stack([count_term, keep_block * (square_down + square_up), flag_value])
    for bit in col_bits:
        scalars = scalars + swap(scalars, "col", bit)
    hops = list(row_bits)

    model = w_up.shape[0]
    parts = 3 if model % (3 * TILE) == 0 else 1
    step = model // parts
    stages = []
    operand = after(hidden_all, scalars)
    for part in range(parts):
        product = lax.dot_general(
            operand, w_up[part * step : (part + 1) * step], LAST, preferred_element_type=F32
        )
        mine, theirs = sides(product)
        for bit in hops[:1] if part < parts - 1 else hops:
            scalars = scalars + swap(scalars, "row", bit)
        hops = hops[1:]
        theirs = after(theirs.astype(BF16), scalars)
        total = mine + swap(theirs, "row", 1).astype(F32)
        stages.append([total])
        for bit in row_bits[1:]:
            split = total.shape[0] // 2
            total = total[:split] + swap(total[split:].astype(BF16), "row", bit).astype(F32)
            stages[-1].append(total)
        operand = after(operand, theirs)
    count_all, square_all, flag_all = scalars[0], jnp.maximum(scalars[1], 0.0), scalars[2]

    token_total = jnp.maximum(count_all, 1.0)
    squares = square_all / (token_total * token_total)
    block_count = float(n_row * n_col)
    estimate = squares * block_count / jnp.maximum(block_count - flag_all, 1.0)
    limit = 0.25 * math.sqrt(
        (w_up.shape[1] * n_row) * (w_up.shape[0] * n_col) / tokens
    )
    clip_factor = jnp.minimum(1.0, limit / jnp.sqrt(estimate + 1e-06))
    scale = keep_block * clip_factor / token_total

    def gradient(left, right, scale):
        product = lax.dot_general(left, right, FIRST, preferred_element_type=F32)
        return (product * scale).astype(BF16)

    grad_down = gradient(act, masked_all, after(scale, *[stage[0] for stage in stages[:-1]]))
    events = [stage[1] for stage in stages[:-1]] + [stages[-1][0], grad_down]
    grad_up = gradient(inputs_all, hidden_all, after(scale, *events))
    input_sum = jnp.concatenate([stage[-1] for stage in stages], axis=1)
    return (input_sum / token_total).astype(BF16), grad_up, grad_down


def solution(mesh):
    placed = (
        P("row", "col"),
        P("col", "row"),
        P("row", "col"),
        P("row"),
        P("row", "col"),
        P("col", "row"),
        P("row", "col"),
    )
    return jax.shard_map(
        on_device,
        mesh=mesh,
        in_specs=placed,
        out_specs=(P("row", "col"), P("col", "row"), P("row", "col")),
        check_vma=False,
    )
```

```python
import math

import jax
import jax.numpy as jnp
from jax import lax
from jax.experimental import pallas as pl
from jax.experimental.pallas import tpu as pltpu
from jax.sharding import PartitionSpec as P

F32 = jnp.float32
BF16 = jnp.bfloat16
LAST = (((1,), (1,)), ((), ()))
FIRST = (((0,), (0,)), ((), ()))
FACTOR = math.sqrt(2.0 / math.pi)
TILE = 256
VMEM_LIMIT = 56 * 1024 * 1024


def swap(value, axis, bit):
    size = lax.axis_size(axis)
    return lax.ppermute(value, axis, [(i, i ^ bit) for i in range(size)])


def bits_of(size):
    return [1 << i for i in range(size.bit_length() - 1)]


def turned(index, size):
    return sum(((index // bit) % 2) * (size // 2 // bit) for bit in bits_of(size))


def call(kernel, grid, in_specs, out_specs, out_shape, moved):
    return pl.pallas_call(
        kernel,
        grid_spec=pltpu.PrefetchScalarGridSpec(
            num_scalar_prefetch=1,
            grid=grid,
            in_specs=in_specs,
            out_specs=out_specs,
        ),
        out_shape=out_shape,
        compiler_params=pltpu.CompilerParams(
            dimension_semantics=("arbitrary",), vmem_limit_bytes=VMEM_LIMIT
        ),
        cost_estimate=pl.CostEstimate(
            flops=1000, bytes_accessed=moved, transcendentals=0
        ),
    )


def whole_index(i, flags):
    return (0, 0)


def column_index(i, flags):
    return (0, i)


def aligned(start):
    return pl.multiple_of(start, 16)


def token_place(index, core, per_group):
    group, k = index // 2 // per_group, index // 2 % per_group
    return (2 * group + (index % 2 ^ core)) * per_group + k


def widest(width, limit):
    return max(tile for tile in range(128, limit + 1, 128) if width % tile == 0)


def gelu_all(pieces, offsets, flags, n_row, per_group, rows):
    width = pieces[0].shape[1]
    per_col = pieces[0].shape[0] // rows
    tokens = n_row * rows
    tile = widest(width, 256)

    def kernel(flags_ref, *refs):
        act_ref, slope_ref = refs[-2:]
        row, core, col = flags_ref[0], flags_ref[1], flags_ref[2]
        for ref, offset in zip(refs[:-2], offsets):
            for part in range(per_col):
                index = row ^ ((col ^ offset) * per_col + part)
                hval = ref[part * rows : (part + 1) * rows, :].astype(F32)
                tanh_part = jnp.tanh(FACTOR * (hval + 0.044715 * hval * hval * hval))
                place = token_place(index, core, per_group)
                act_ref[pl.ds(aligned(place * rows), rows), :] = (
                    0.5 * hval * (1.0 + tanh_part)
                ).astype(BF16)

                @pl.when(index % 2 == core)
                def _():
                    slope_ref[pl.ds(aligned((index // 2) * rows), rows), :] = 0.5 * (
                        1.0 + tanh_part
                    ) + 0.5 * hval * (1.0 - tanh_part * tanh_part) * FACTOR * (
                        1.0 + 3.0 * 0.044715 * hval * hval
                    )

    return call(
        kernel,
        (width // tile,),
        [pl.BlockSpec((piece.shape[0], tile), column_index) for piece in pieces],
        [
            pl.BlockSpec((tokens, tile), column_index),
            pl.BlockSpec((tokens // 2, tile), column_index),
        ],
        [
            jax.ShapeDtypeStruct((tokens, width), BF16),
            jax.ShapeDtypeStruct((tokens // 2, width), F32),
        ],
        24 * tokens * width,
    )(flags, *pieces)


def arrange(pieces, places, rows, flags):
    width = pieces[0].shape[1]
    tokens = sum(piece.shape[0] for piece in pieces)
    tile = widest(width, width // 2)

    def kernel(flags_ref, *refs):
        for ref, blocks in zip(refs, places):
            for k, place in enumerate(blocks):
                start = aligned(place(flags_ref[1]) * rows)
                refs[-1][pl.ds(start, rows), :] = ref[k * rows : (k + 1) * rows, :]

    return call(
        kernel,
        (width // tile,),
        [pl.BlockSpec((piece.shape[0], tile), column_index) for piece in pieces],
        pl.BlockSpec((tokens, tile), column_index),
        jax.ShapeDtypeStruct((tokens, width), BF16),
        6 * tokens * width,
    )(flags, *pieces)


def gram(value):
    return lax.dot_general(value, value, LAST, preferred_element_type=F32)


def after(value, *events):
    return lax.optimization_barrier((value, *events))[0]


def on_device(inputs, pre_act, out_grad, token_valid, poison, w_up, w_down):
    n_row = lax.axis_size("row")
    n_col = lax.axis_size("col")
    rows = inputs.shape[0]
    tokens = rows * n_row
    slots = n_row // 2
    row, col = lax.axis_index("row"), lax.axis_index("col")
    core = col % 2
    flags = jnp.stack([row, core, col]).astype(jnp.int32)
    row_bits, col_bits = bits_of(n_row), bits_of(n_col)

    def first_hops(own, x_own, near_first):
        blocks = {0: own}
        for bit in row_bits:
            source = x_own if bit == 1 else own
            if near_first and bit == row_bits[-1]:
                source = after(source, blocks[1], blocks[2])
            blocks[bit] = swap(source, "row", bit)
        return blocks

    def other_hops(blocks, *events):
        blocks = dict(blocks)
        for bit in reversed(row_bits[1:]):
            for index in sorted(blocks):
                if index > 0 and index % (2 * bit) == 0:
                    blocks[index | bit] = swap(after(blocks[index], *events), "row", bit)
        for index in sorted(blocks):
            if index > 0 and index % 2 == 0:
                blocks[index | 1] = swap(after(blocks[index], *events), "row", 1)
        return [blocks[index] for index in range(n_row)]

    groups = 2 if slots % 2 == 0 else 1
    per_group = slots // groups
    count = per_group * rows
    by_group = [range(2 * g * per_group, 2 * (g + 1) * per_group) for g in range(groups)]

    pieces, offsets = [pre_act], [0]
    for bit in reversed(col_bits):
        pieces = pieces + [swap(piece, "col", bit) for piece in pieces]
        offsets = offsets + [offset ^ bit for offset in offsets]

    own = out_grad * token_valid.astype(BF16)[:, None]
    masked = other_hops(first_hops(own, own, True))
    own = after(inputs, masked[-2])
    inputs_hops = first_hops(own, after(own, masked[-1]), False)

    blocks, totals, received = [], [], []
    for group, indices in enumerate(by_group):
        base = 2 * group * per_group
        block = arrange(
            [masked[index] for index in indices],
            [
                [lambda core, i=index, b=base: token_place(i, core, per_group) - b]
                for index in indices
            ],
            rows,
            flags,
        )
        blocks.append(block)
        if group == 0:
            first, second = [], [masked[n_row // 2], pieces[1]]
        else:
            act, slope = gelu_all(
                [after(pieces[0], masked[-2], masked[n_row // 2 + 1], *totals)] + pieces[1:],
                offsets,
                flags,
                n_row,
                per_group,
                rows,
            )
            inputs_blocks = other_hops(inputs_hops, act)
            first = received + [act, inputs_hops[1]]
            second = [inputs_blocks[n_row // 2 + 1], inputs_blocks[n_row - 2]]
        partial = lax.dot_general(
            after(block, *first), w_down, LAST, preferred_element_type=F32
        )
        total = partial[:count]
        got = swap(after(partial[count:].astype(BF16), *second), "col", 1)
        for bit in col_bits[1:]:
            total = total + got.astype(F32)
            got = swap(total.astype(BF16), "col", bit)
        totals.append(total)
        received.append(got)
    masked_all = arrange(
        blocks,
        [
            [lambda core, p=p: p for p in range(2 * g * per_group, 2 * (g + 1) * per_group)]
            for g in range(groups)
        ],
        rows,
        flags,
    )
    masked_gram = gram(after(masked_all, inputs_blocks[3]))
    square_down = jnp.sum(masked_gram * gram(after(act, masked_gram)))

    def exchange_place(side, slot, swapped):
        return lambda core: (side ^ (core & swapped)) * slots + turned(slot, slots)

    inputs_all = arrange(
        [after(inputs_blocks[0], square_down)] + inputs_blocks[1:],
        [[exchange_place(index % 2, index // 2, 0)] for index in range(n_row)],
        rows,
        flags,
    )
    inputs_gram = gram(inputs_all)
    hidden_blocks = []
    for group, (total, got) in enumerate(zip(totals, received)):
        if hidden_blocks:
            got = after(got, hidden_blocks[-1], square_down)
        total = total + got.astype(F32)
        hidden = (total * slope[group * count : (group + 1) * count]).astype(BF16)
        hidden_blocks += [hidden, swap(hidden, "col", 1)]
    hidden_blocks[-1] = after(hidden_blocks[-1], inputs_gram)
    hidden_all = arrange(
        hidden_blocks,
        [
            [exchange_place(side, g * per_group + k, 1) for k in range(per_group)]
            for g in range(groups)
            for side in range(2)
        ],
        rows,
        flags,
    )

    flag_value = poison[0, 0].astype(F32)
    keep_block = 1.0 - flag_value
    count_term = jnp.where(col == 0, jnp.sum(token_valid.astype(F32)), 0.0)

    square_up = jnp.sum(inputs_gram * gram(hidden_all))
    scalars = jnp.stack([count_term, keep_block * (square_down + square_up), flag_value])
    for bit in col_bits:
        scalars = scalars + swap(scalars, "col", bit)
    hops = list(row_bits)

    model = w_up.shape[0]
    parts = 3 if model % (3 * TILE) == 0 else 1
    step = model // parts
    stages = []
    operand = after(hidden_all, scalars)
    for part in range(parts):
        product = lax.dot_general(
            operand, w_up[part * step : (part + 1) * step], LAST, preferred_element_type=F32
        )
        mine, theirs = product[: tokens // 2], product[tokens // 2 :]
        for bit in hops[:1] if part < parts - 1 else hops:
            scalars = scalars + swap(scalars, "row", bit)
        hops = hops[1:]
        theirs = after(theirs.astype(BF16), scalars)
        total = mine + swap(theirs, "row", 1).astype(F32)
        stages.append([total])
        for bit in row_bits[1:]:
            split = total.shape[0] // 2
            total = total[:split] + swap(total[split:].astype(BF16), "row", bit).astype(F32)
            stages[-1].append(total)
        operand = after(operand, theirs)
    count_all, square_all, flag_all = scalars[0], jnp.maximum(scalars[1], 0.0), scalars[2]

    token_total = jnp.maximum(count_all, 1.0)
    squares = square_all / (token_total * token_total)
    block_count = float(n_row * n_col)
    estimate = squares * block_count / jnp.maximum(block_count - flag_all, 1.0)
    limit = 0.25 * math.sqrt(
        (w_up.shape[1] * n_row) * (w_up.shape[0] * n_col) / tokens
    )
    clip_factor = jnp.minimum(1.0, limit / jnp.sqrt(estimate + 1e-06))
    scale = keep_block * clip_factor / token_total

    def gradient(left, right, scale):
        product = lax.dot_general(left, right, FIRST, preferred_element_type=F32)
        return (product * scale).astype(BF16)

    grad_down = gradient(act, masked_all, after(scale, *[stage[0] for stage in stages[:-1]]))
    events = [stage[1] for stage in stages[:-1]] + [stages[-1][0], grad_down]
    grad_up = gradient(inputs_all, hidden_all, after(scale, *events))
    input_sum = jnp.concatenate([stage[-1] for stage in stages], axis=1)
    return (input_sum / token_total).astype(BF16), grad_up, grad_down


def solution(mesh):
    placed = (
        P("row", "col"),
        P("col", "row"),
        P("row", "col"),
        P("row"),
        P("row", "col"),
        P("col", "row"),
        P("row", "col"),
    )
    return jax.shard_map(
        on_device,
        mesh=mesh,
        in_specs=placed,
        out_specs=(P("row", "col"), P("col", "row"), P("row", "col")),
        check_vma=False,
    )
```

```python
import math

import jax
import jax.numpy as jnp
from jax import lax
from jax.experimental import pallas as pl
from jax.experimental.pallas import tpu as pltpu
from jax.sharding import PartitionSpec as P

F32 = jnp.float32
BF16 = jnp.bfloat16
LAST = (((1,), (1,)), ((), ()))
FIRST = (((0,), (0,)), ((), ()))
FACTOR = math.sqrt(2.0 / math.pi)
TILE = 256
VMEM_LIMIT = 56 * 1024 * 1024


def swap(value, axis, bit):
    size = lax.axis_size(axis)
    return lax.ppermute(value, axis, [(i, i ^ bit) for i in range(size)])


def bits_of(size):
    return [1 << i for i in range(size.bit_length() - 1)]


def turned(index, size):
    return sum(((index // bit) % 2) * (size // 2 // bit) for bit in bits_of(size))


def call(kernel, grid, in_specs, out_specs, out_shape, moved):
    return pl.pallas_call(
        kernel,
        grid_spec=pltpu.PrefetchScalarGridSpec(
            num_scalar_prefetch=1,
            grid=grid,
            in_specs=in_specs,
            out_specs=out_specs,
        ),
        out_shape=out_shape,
        compiler_params=pltpu.CompilerParams(
            dimension_semantics=("arbitrary",), vmem_limit_bytes=VMEM_LIMIT
        ),
        cost_estimate=pl.CostEstimate(
            flops=1000, bytes_accessed=moved, transcendentals=0
        ),
    )


def whole_index(i, flags):
    return (0, 0)


def column_index(i, flags):
    return (0, i)


def aligned(start):
    return pl.multiple_of(start, 16)


def token_place(index, core, per_group):
    group, k = index // 2 // per_group, index // 2 % per_group
    return (2 * group + (index % 2 ^ core)) * per_group + k


def widest(width, limit):
    return max(tile for tile in range(128, limit + 1, 128) if width % tile == 0)


def gelu_all(pieces, offsets, flags, n_row, per_group, rows):
    width = pieces[0].shape[1]
    per_col = pieces[0].shape[0] // rows
    tokens = n_row * rows
    tile = widest(width, 256)

    def kernel(flags_ref, *refs):
        act_ref, slope_ref = refs[-2:]
        row, core, col = flags_ref[0], flags_ref[1], flags_ref[2]
        for ref, offset in zip(refs[:-2], offsets):
            for part in range(per_col):
                index = row ^ ((col ^ offset) * per_col + part)
                hval = ref[part * rows : (part + 1) * rows, :].astype(F32)
                tanh_part = jnp.tanh(FACTOR * (hval + 0.044715 * hval * hval * hval))
                place = token_place(index, core, per_group)
                act_ref[pl.ds(aligned(place * rows), rows), :] = (
                    0.5 * hval * (1.0 + tanh_part)
                ).astype(BF16)

                @pl.when(index % 2 == core)
                def _():
                    slope_ref[pl.ds(aligned((index // 2) * rows), rows), :] = 0.5 * (
                        1.0 + tanh_part
                    ) + 0.5 * hval * (1.0 - tanh_part * tanh_part) * FACTOR * (
                        1.0 + 3.0 * 0.044715 * hval * hval
                    )

    return call(
        kernel,
        (width // tile,),
        [pl.BlockSpec((piece.shape[0], tile), column_index) for piece in pieces],
        [
            pl.BlockSpec((tokens, tile), column_index),
            pl.BlockSpec((tokens // 2, tile), column_index),
        ],
        [
            jax.ShapeDtypeStruct((tokens, width), BF16),
            jax.ShapeDtypeStruct((tokens // 2, width), F32),
        ],
        24 * tokens * width,
    )(flags, *pieces)


def arrange(pieces, places, rows, flags):
    width = pieces[0].shape[1]
    tokens = sum(piece.shape[0] for piece in pieces)
    tile = widest(width, width // 2)

    def kernel(flags_ref, *refs):
        for ref, blocks in zip(refs, places):
            for k, place in enumerate(blocks):
                start = aligned(place(flags_ref[1]) * rows)
                refs[-1][pl.ds(start, rows), :] = ref[k * rows : (k + 1) * rows, :]

    return call(
        kernel,
        (width // tile,),
        [pl.BlockSpec((piece.shape[0], tile), column_index) for piece in pieces],
        pl.BlockSpec((tokens, tile), column_index),
        jax.ShapeDtypeStruct((tokens, width), BF16),
        6 * tokens * width,
    )(flags, *pieces)


def gram(value):
    return lax.dot_general(value, value, LAST, preferred_element_type=F32)


def after(value, *events):
    return lax.optimization_barrier((value, *events))[0]


def on_device(inputs, pre_act, out_grad, token_valid, poison, w_up, w_down):
    n_row = lax.axis_size("row")
    n_col = lax.axis_size("col")
    rows = inputs.shape[0]
    tokens = rows * n_row
    slots = n_row // 2
    row, col = lax.axis_index("row"), lax.axis_index("col")
    core = col % 2
    flags = jnp.stack([row, core, col]).astype(jnp.int32)
    row_bits, col_bits = bits_of(n_row), bits_of(n_col)

    def first_hops(own, x_own, near_first):
        blocks = {0: own}
        for bit in row_bits:
            source = x_own if bit == 1 else own
            if near_first and bit == row_bits[-1]:
                source = after(source, blocks[1], blocks[2])
            blocks[bit] = swap(source, "row", bit)
        return blocks

    def other_hops(blocks, events=(), late=()):
        near, blocks = blocks, dict(blocks)
        for bit in reversed(row_bits[1:]):
            for index in sorted(blocks):
                if index > 0 and index % (2 * bit) == 0:
                    blocks[index | bit] = swap(after(blocks[index], *events), "row", bit)
        for index in sorted(blocks):
            if index > 0 and index % 2 == 0:
                source = after(blocks[index], *(events if index in near else late))
                blocks[index | 1] = swap(source, "row", 1)
        return [blocks[index] for index in range(n_row)]

    groups = 2 if slots % 2 == 0 else 1
    per_group = slots // groups
    count = per_group * rows
    by_group = [range(2 * g * per_group, 2 * (g + 1) * per_group) for g in range(groups)]

    pieces, offsets = [pre_act], [0]
    for bit in reversed(col_bits):
        pieces = pieces + [swap(piece, "col", bit) for piece in pieces]
        offsets = offsets + [offset ^ bit for offset in offsets]

    own = out_grad * token_valid.astype(BF16)[:, None]
    masked = other_hops(first_hops(own, own, True))
    own = after(inputs, masked[-2])

    blocks, totals, received = [], [], []
    for group, indices in enumerate(by_group):
        if group == 1:
            act, slope = gelu_all(
                [after(pieces[0], *totals)] + pieces[1:],
                offsets,
                flags,
                n_row,
                per_group,
                rows,
            )
            masked[-1] = swap(after(masked[-2], act), "row", 1)
            inputs_hops = first_hops(own, after(own, masked[-1]), False)
        base = 2 * group * per_group
        block = arrange(
            [masked[index] for index in indices],
            [
                [lambda core, i=index, b=base: token_place(i, core, per_group) - b]
                for index in indices
            ],
            rows,
            flags,
        )
        blocks.append(block)
        if group == 0:
            first, second = [], [masked[n_row // 2], pieces[1]]
        else:
            first = received + [inputs_hops[1]]
            second = [inputs_hops[2], inputs_hops[n_row // 2]]
        partial = lax.dot_general(
            after(block, *first), w_down, LAST, preferred_element_type=F32
        )
        total = partial[:count]
        got = swap(after(partial[count:].astype(BF16), *second), "col", 1)
        for bit in col_bits[1:]:
            total = total + got.astype(F32)
            got = swap(total.astype(BF16), "col", bit)
        totals.append(total)
        received.append(got)
    masked_all = arrange(
        [after(blocks[0], total)] + blocks[1:],
        [
            [lambda core, p=p: p for p in range(2 * g * per_group, 2 * (g + 1) * per_group)]
            for g in range(groups)
        ],
        rows,
        flags,
    )
    masked_gram = gram(masked_all)
    inputs_blocks = other_hops(inputs_hops, [partial], [masked_gram])
    hidden_blocks = []
    for group, (total, got) in enumerate(zip(totals, received)):
        if hidden_blocks:
            got = after(got, hidden_blocks[-1], masked_gram)
        total = total + got.astype(F32)
        hidden = (total * slope[group * count : (group + 1) * count]).astype(BF16)
        hidden_blocks += [hidden, swap(hidden, "col", 1)]
    square_down = jnp.sum(masked_gram * gram(after(act, hidden)))

    def exchange_place(side, slot, swapped):
        return lambda core: (side ^ (core & swapped)) * slots + turned(slot, slots)

    inputs_all = arrange(
        [after(inputs_blocks[0], square_down)] + inputs_blocks[1:],
        [[exchange_place(index % 2, index // 2, 0)] for index in range(n_row)],
        rows,
        flags,
    )
    inputs_gram = gram(inputs_all)
    hidden_blocks[-1] = after(hidden_blocks[-1], inputs_gram)
    hidden_all = arrange(
        hidden_blocks,
        [
            [exchange_place(side, g * per_group + k, 1) for k in range(per_group)]
            for g in range(groups)
            for side in range(2)
        ],
        rows,
        flags,
    )

    flag_value = poison[0, 0].astype(F32)
    keep_block = 1.0 - flag_value
    count_term = jnp.where(col == 0, jnp.sum(token_valid.astype(F32)), 0.0)

    square_up = jnp.sum(inputs_gram * gram(hidden_all))
    scalars = jnp.stack([count_term, keep_block * (square_down + square_up), flag_value])
    for bit in col_bits:
        scalars = scalars + swap(scalars, "col", bit)
    hops = list(row_bits)

    model = w_up.shape[0]
    parts = 3 if model % (3 * TILE) == 0 else 1
    step = model // parts
    stages = []
    operand = after(hidden_all, scalars)
    for part in range(parts):
        product = lax.dot_general(
            operand, w_up[part * step : (part + 1) * step], LAST, preferred_element_type=F32
        )
        mine, theirs = product[: tokens // 2], product[tokens // 2 :]
        for bit in hops[:1] if part < parts - 1 else hops:
            scalars = scalars + swap(scalars, "row", bit)
        hops = hops[1:]
        theirs = after(theirs.astype(BF16), scalars)
        total = mine + swap(theirs, "row", 1).astype(F32)
        stages.append([total])
        for bit in row_bits[1:]:
            split = total.shape[0] // 2
            total = total[:split] + swap(total[split:].astype(BF16), "row", bit).astype(F32)
            stages[-1].append(total)
        operand = after(operand, theirs)
    count_all, square_all, flag_all = scalars[0], jnp.maximum(scalars[1], 0.0), scalars[2]

    token_total = jnp.maximum(count_all, 1.0)
    squares = square_all / (token_total * token_total)
    block_count = float(n_row * n_col)
    estimate = squares * block_count / jnp.maximum(block_count - flag_all, 1.0)
    limit = 0.25 * math.sqrt(
        (w_up.shape[1] * n_row) * (w_up.shape[0] * n_col) / tokens
    )
    clip_factor = jnp.minimum(1.0, limit / jnp.sqrt(estimate + 1e-06))
    scale = keep_block * clip_factor / token_total

    def gradient(left, right, scale):
        product = lax.dot_general(left, right, FIRST, preferred_element_type=F32)
        return (product * scale).astype(BF16)

    grad_down = gradient(act, masked_all, after(scale, *[stage[0] for stage in stages[:-1]]))
    events = [stage[1] for stage in stages[:-1]] + [stages[-1][0], grad_down]
    grad_up = gradient(inputs_all, hidden_all, after(scale, *events))
    input_sum = jnp.concatenate([stage[-1] for stage in stages], axis=1)
    return (input_sum / token_total).astype(BF16), grad_up, grad_down


def solution(mesh):
    placed = (
        P("row", "col"),
        P("col", "row"),
        P("row", "col"),
        P("row"),
        P("row", "col"),
        P("col", "row"),
        P("row", "col"),
    )
    return jax.shard_map(
        on_device,
        mesh=mesh,
        in_specs=placed,
        out_specs=(P("row", "col"), P("col", "row"), P("row", "col")),
        check_vma=False,
    )
```

```python
import math

import jax
import jax.numpy as jnp
from jax import lax
from jax.experimental import pallas as pl
from jax.experimental.pallas import tpu as pltpu
from jax.sharding import PartitionSpec as P

F32 = jnp.float32
BF16 = jnp.bfloat16
LAST = (((1,), (1,)), ((), ()))
FIRST = (((0,), (0,)), ((), ()))
FACTOR = math.sqrt(2.0 / math.pi)
TILE = 256
VMEM_LIMIT = 56 * 1024 * 1024


def swap(value, axis, bit):
    size = lax.axis_size(axis)
    return lax.ppermute(value, axis, [(i, i ^ bit) for i in range(size)])


def bits_of(size):
    return [1 << i for i in range(size.bit_length() - 1)]


def turned(index, size):
    return sum(((index // bit) % 2) * (size // 2 // bit) for bit in bits_of(size))


def call(kernel, grid, in_specs, out_specs, out_shape, moved):
    return pl.pallas_call(
        kernel,
        grid_spec=pltpu.PrefetchScalarGridSpec(
            num_scalar_prefetch=1,
            grid=grid,
            in_specs=in_specs,
            out_specs=out_specs,
        ),
        out_shape=out_shape,
        compiler_params=pltpu.CompilerParams(
            dimension_semantics=("arbitrary",), vmem_limit_bytes=VMEM_LIMIT
        ),
        cost_estimate=pl.CostEstimate(
            flops=1000, bytes_accessed=moved, transcendentals=0
        ),
    )


def whole_index(i, flags):
    return (0, 0)


def column_index(i, flags):
    return (0, i)


def aligned(start):
    return pl.multiple_of(start, 16)


def token_place(index, core, per_group):
    group, k = index // 2 // per_group, index // 2 % per_group
    return (2 * group + (index % 2 ^ core)) * per_group + k


def widest(width, limit):
    return max(tile for tile in range(128, limit + 1, 128) if width % tile == 0)


def gelu_all(pieces, offsets, flags, n_row, per_group, rows):
    width = pieces[0].shape[1]
    per_col = pieces[0].shape[0] // rows
    tokens = n_row * rows
    tile = widest(width, 256)

    def kernel(flags_ref, *refs):
        act_ref, slope_ref = refs[-2:]
        row, core, col = flags_ref[0], flags_ref[1], flags_ref[2]
        for ref, offset in zip(refs[:-2], offsets):
            for part in range(per_col):
                index = row ^ ((col ^ offset) * per_col + part)
                hval = ref[part * rows : (part + 1) * rows, :].astype(F32)
                tanh_part = jnp.tanh(FACTOR * (hval + 0.044715 * hval * hval * hval))
                place = token_place(index, core, per_group)
                act_ref[pl.ds(aligned(place * rows), rows), :] = (
                    0.5 * hval * (1.0 + tanh_part)
                ).astype(BF16)

                @pl.when(index % 2 == core)
                def _():
                    slope_ref[pl.ds(aligned((index // 2) * rows), rows), :] = 0.5 * (
                        1.0 + tanh_part
                    ) + 0.5 * hval * (1.0 - tanh_part * tanh_part) * FACTOR * (
                        1.0 + 3.0 * 0.044715 * hval * hval
                    )

    return call(
        kernel,
        (width // tile,),
        [pl.BlockSpec((piece.shape[0], tile), column_index) for piece in pieces],
        [
            pl.BlockSpec((tokens, tile), column_index),
            pl.BlockSpec((tokens // 2, tile), column_index),
        ],
        [
            jax.ShapeDtypeStruct((tokens, width), BF16),
            jax.ShapeDtypeStruct((tokens // 2, width), F32),
        ],
        24 * tokens * width,
    )(flags, *pieces)


def arrange(pieces, places, rows, flags):
    width = pieces[0].shape[1]
    tokens = sum(piece.shape[0] for piece in pieces)
    tile = widest(width, width // 2)

    def kernel(flags_ref, *refs):
        for ref, blocks in zip(refs, places):
            for k, place in enumerate(blocks):
                start = aligned(place(flags_ref[1]) * rows)
                refs[-1][pl.ds(start, rows), :] = ref[k * rows : (k + 1) * rows, :]

    return call(
        kernel,
        (width // tile,),
        [pl.BlockSpec((piece.shape[0], tile), column_index) for piece in pieces],
        pl.BlockSpec((tokens, tile), column_index),
        jax.ShapeDtypeStruct((tokens, width), BF16),
        6 * tokens * width,
    )(flags, *pieces)


def gram(value):
    return lax.dot_general(value, value, LAST, preferred_element_type=F32)


def after(value, *events):
    return lax.optimization_barrier((value, *events))[0]


def on_device(inputs, pre_act, out_grad, token_valid, poison, w_up, w_down):
    n_row = lax.axis_size("row")
    n_col = lax.axis_size("col")
    rows = inputs.shape[0]
    tokens = rows * n_row
    slots = n_row // 2
    row, col = lax.axis_index("row"), lax.axis_index("col")
    core = col % 2
    flags = jnp.stack([row, core, col]).astype(jnp.int32)
    row_bits, col_bits = bits_of(n_row), bits_of(n_col)

    def first_hops(own, x_own, near_first):
        blocks = {0: own}
        for bit in row_bits:
            source = x_own if bit == 1 else own
            if near_first and bit == row_bits[-1]:
                source = after(source, blocks[1], blocks[2])
            blocks[bit] = swap(source, "row", bit)
        return blocks

    def other_hops(blocks, events=(), late=()):
        near, blocks = blocks, dict(blocks)
        for bit in reversed(row_bits[1:]):
            for index in sorted(blocks):
                if index > 0 and index % (2 * bit) == 0:
                    blocks[index | bit] = swap(after(blocks[index], *events), "row", bit)
        for index in sorted(blocks):
            if index > 0 and index % 2 == 0:
                source = after(blocks[index], *(events if index in near else late))
                blocks[index | 1] = swap(source, "row", 1)
        return [blocks[index] for index in range(n_row)]

    groups = 2 if slots % 2 == 0 else 1
    per_group = slots // groups
    count = per_group * rows
    by_group = [range(2 * g * per_group, 2 * (g + 1) * per_group) for g in range(groups)]

    pieces, offsets = [pre_act], [0]
    for bit in reversed(col_bits):
        pieces = pieces + [swap(piece, "col", bit) for piece in pieces]
        offsets = offsets + [offset ^ bit for offset in offsets]

    own = out_grad * token_valid.astype(BF16)[:, None]
    masked = other_hops(first_hops(own, own, True))
    own = after(inputs, masked[-2])

    blocks, totals, received = [], [], []
    for group, indices in enumerate(by_group):
        if group == 1:
            act, slope = gelu_all(
                [after(pieces[0], *totals)] + pieces[1:],
                offsets,
                flags,
                n_row,
                per_group,
                rows,
            )
            masked[-1] = swap(after(masked[-2], act, masked[n_row // 2 + 1]), "row", 1)
            inputs_hops = first_hops(own, after(own, masked[-1]), False)
        base = 2 * group * per_group
        block = arrange(
            [masked[index] for index in indices],
            [
                [lambda core, i=index, b=base: token_place(i, core, per_group) - b]
                for index in indices
            ],
            rows,
            flags,
        )
        blocks.append(block)
        if group == 0:
            first, second = [], [masked[n_row // 2], pieces[1]]
        else:
            first = received
            second = [inputs_hops[bit] for bit in row_bits]
        partial = lax.dot_general(
            after(block, *first), w_down, LAST, preferred_element_type=F32
        )
        total = partial[:count]
        got = swap(after(partial[count:].astype(BF16), *second), "col", 1)
        for bit in col_bits[1:]:
            total = total + got.astype(F32)
            got = swap(total.astype(BF16), "col", bit)
        totals.append(total)
        received.append(got)
    masked_all = arrange(
        [after(blocks[0], total)] + blocks[1:],
        [
            [lambda core, p=p: p for p in range(2 * g * per_group, 2 * (g + 1) * per_group)]
            for g in range(groups)
        ],
        rows,
        flags,
    )
    masked_gram = gram(masked_all)
    inputs_blocks = other_hops(inputs_hops, [partial], [masked_gram])
    hidden_blocks = []
    for group, (total, got) in enumerate(zip(totals, received)):
        if hidden_blocks:
            got = after(got, hidden_blocks[-1], masked_gram)
        total = total + got.astype(F32)
        hidden = (total * slope[group * count : (group + 1) * count]).astype(BF16)
        hidden_blocks += [hidden, swap(hidden, "col", 1)]
    square_down = jnp.sum(masked_gram * gram(after(act, hidden)))

    def exchange_place(side, slot, swapped):
        return lambda core: (side ^ (core & swapped)) * slots + turned(slot, slots)

    inputs_all = arrange(
        [after(inputs_blocks[0], square_down)] + inputs_blocks[1:],
        [[exchange_place(index % 2, index // 2, 0)] for index in range(n_row)],
        rows,
        flags,
    )
    inputs_gram = gram(inputs_all)
    hidden_blocks[-1] = after(hidden_blocks[-1], inputs_gram)
    hidden_all = arrange(
        hidden_blocks,
        [
            [exchange_place(side, g * per_group + k, 1) for k in range(per_group)]
            for g in range(groups)
            for side in range(2)
        ],
        rows,
        flags,
    )

    flag_value = poison[0, 0].astype(F32)
    keep_block = 1.0 - flag_value
    count_term = jnp.where(col == 0, jnp.sum(token_valid.astype(F32)), 0.0)

    col_hops, row_hops = list(col_bits), list(row_bits)

    model = w_up.shape[0]
    parts = 3 if model % (3 * TILE) == 0 else 1
    step = model // parts
    stages = []
    operand = hidden_all
    for part in range(parts):
        product = lax.dot_general(
            operand, w_up[part * step : (part + 1) * step], LAST, preferred_element_type=F32
        )
        mine, theirs = product[: tokens // 2], product[tokens // 2 :].astype(BF16)
        if part > 0:
            for bit in col_hops:
                scalars = scalars + swap(scalars, "col", bit)
            if part == 1:
                scalars = after(scalars, stages[0][0])
            for bit in row_hops[:1]:
                scalars = scalars + swap(scalars, "row", bit)
            col_hops, row_hops = [], row_hops[1:]
            theirs = after(theirs, scalars)
        total = mine + swap(theirs, "row", 1).astype(F32)
        stages.append([total])
        for bit in row_bits[1:]:
            split = total.shape[0] // 2
            total = total[:split] + swap(total[split:].astype(BF16), "row", bit).astype(F32)
            stages[-1].append(total)
        if part == 0:
            square_up = jnp.sum(inputs_gram * gram(after(hidden_all, theirs)))
            scalars = jnp.stack(
                [count_term, keep_block * (square_down + square_up), flag_value]
            )
            scalars = scalars + swap(scalars, "col", col_hops.pop(0))
            operand = after(hidden_all, scalars)
        else:
            operand = after(operand, theirs)
    for axis, bits in (("col", col_hops), ("row", row_hops)):
        for bit in bits:
            scalars = scalars + swap(scalars, axis, bit)
    count_all, square_all, flag_all = scalars[0], jnp.maximum(scalars[1], 0.0), scalars[2]

    token_total = jnp.maximum(count_all, 1.0)
    squares = square_all / (token_total * token_total)
    block_count = float(n_row * n_col)
    estimate = squares * block_count / jnp.maximum(block_count - flag_all, 1.0)
    limit = 0.25 * math.sqrt(
        (w_up.shape[1] * n_row) * (w_up.shape[0] * n_col) / tokens
    )
    clip_factor = jnp.minimum(1.0, limit / jnp.sqrt(estimate + 1e-06))
    scale = keep_block * clip_factor / token_total

    def gradient(left, right, scale):
        product = lax.dot_general(left, right, FIRST, preferred_element_type=F32)
        return (product * scale).astype(BF16)

    grad_down = gradient(act, masked_all, after(scale, *[stage[0] for stage in stages[:-1]]))
    events = [stage[1] for stage in stages[:-1]] + [stages[-1][0], grad_down]
    grad_up = gradient(inputs_all, hidden_all, after(scale, *events))
    input_sum = jnp.concatenate([stage[-1] for stage in stages], axis=1)
    return (input_sum / token_total).astype(BF16), grad_up, grad_down


def solution(mesh):
    placed = (
        P("row", "col"),
        P("col", "row"),
        P("row", "col"),
        P("row"),
        P("row", "col"),
        P("col", "row"),
        P("row", "col"),
    )
    return jax.shard_map(
        on_device,
        mesh=mesh,
        in_specs=placed,
        out_specs=(P("row", "col"), P("col", "row"), P("row", "col")),
        check_vma=False,
    )
```

```python
import math

import jax
import jax.numpy as jnp
from jax import lax
from jax.experimental import pallas as pl
from jax.experimental.pallas import tpu as pltpu
from jax.sharding import PartitionSpec as P

F32 = jnp.float32
BF16 = jnp.bfloat16
LAST = (((1,), (1,)), ((), ()))
FIRST = (((0,), (0,)), ((), ()))
FACTOR = math.sqrt(2.0 / math.pi)
TILE = 256
VMEM_LIMIT = 56 * 1024 * 1024


def swap(value, axis, bit):
    size = lax.axis_size(axis)
    return lax.ppermute(value, axis, [(i, i ^ bit) for i in range(size)])


def bits_of(size):
    return [1 << i for i in range(size.bit_length() - 1)]


def turned(index, size):
    return sum(((index // bit) % 2) * (size // 2 // bit) for bit in bits_of(size))


def call(kernel, grid, in_specs, out_specs, out_shape, moved):
    return pl.pallas_call(
        kernel,
        grid_spec=pltpu.PrefetchScalarGridSpec(
            num_scalar_prefetch=1,
            grid=grid,
            in_specs=in_specs,
            out_specs=out_specs,
        ),
        out_shape=out_shape,
        compiler_params=pltpu.CompilerParams(
            dimension_semantics=("arbitrary",), vmem_limit_bytes=VMEM_LIMIT
        ),
        cost_estimate=pl.CostEstimate(
            flops=1000, bytes_accessed=moved, transcendentals=0
        ),
    )


def whole_index(i, flags):
    return (0, 0)


def column_index(i, flags):
    return (0, i)


def aligned(start):
    return pl.multiple_of(start, 16)


def token_place(index, core, per_group):
    group, k = index // 2 // per_group, index // 2 % per_group
    return (2 * group + (index % 2 ^ core)) * per_group + k


def widest(width, limit):
    return max(tile for tile in range(128, limit + 1, 128) if width % tile == 0)


def gelu_all(pieces, offsets, flags, n_row, per_group, rows):
    width = pieces[0].shape[1]
    per_col = pieces[0].shape[0] // rows
    tokens = n_row * rows
    tile = widest(width, 256)

    def kernel(flags_ref, *refs):
        act_ref, slope_ref = refs[-2:]
        row, core, col = flags_ref[0], flags_ref[1], flags_ref[2]
        for ref, offset in zip(refs[:-2], offsets):
            for part in range(per_col):
                index = row ^ ((col ^ offset) * per_col + part)
                hval = ref[part * rows : (part + 1) * rows, :].astype(F32)
                tanh_part = jnp.tanh(FACTOR * (hval + 0.044715 * hval * hval * hval))
                place = token_place(index, core, per_group)
                act_ref[pl.ds(aligned(place * rows), rows), :] = (
                    0.5 * hval * (1.0 + tanh_part)
                ).astype(BF16)

                @pl.when(index % 2 == core)
                def _():
                    slope_ref[pl.ds(aligned((index // 2) * rows), rows), :] = 0.5 * (
                        1.0 + tanh_part
                    ) + 0.5 * hval * (1.0 - tanh_part * tanh_part) * FACTOR * (
                        1.0 + 3.0 * 0.044715 * hval * hval
                    )

    return call(
        kernel,
        (width // tile,),
        [pl.BlockSpec((piece.shape[0], tile), column_index) for piece in pieces],
        [
            pl.BlockSpec((tokens, tile), column_index),
            pl.BlockSpec((tokens // 2, tile), column_index),
        ],
        [
            jax.ShapeDtypeStruct((tokens, width), BF16),
            jax.ShapeDtypeStruct((tokens // 2, width), F32),
        ],
        24 * tokens * width,
    )(flags, *pieces)


def arrange(pieces, places, rows, flags):
    width = pieces[0].shape[1]
    tokens = sum(piece.shape[0] for piece in pieces)
    tile = widest(width, width // 2)

    def kernel(flags_ref, *refs):
        for ref, blocks in zip(refs, places):
            for k, place in enumerate(blocks):
                start = aligned(place(flags_ref[1]) * rows)
                refs[-1][pl.ds(start, rows), :] = ref[k * rows : (k + 1) * rows, :]

    return call(
        kernel,
        (width // tile,),
        [pl.BlockSpec((piece.shape[0], tile), column_index) for piece in pieces],
        pl.BlockSpec((tokens, tile), column_index),
        jax.ShapeDtypeStruct((tokens, width), BF16),
        6 * tokens * width,
    )(flags, *pieces)


def gram(value):
    return lax.dot_general(value, value, LAST, preferred_element_type=F32)


def after(value, *events):
    return lax.optimization_barrier((value, *events))[0]


def on_device(inputs, pre_act, out_grad, token_valid, poison, w_up, w_down):
    n_row = lax.axis_size("row")
    n_col = lax.axis_size("col")
    rows = inputs.shape[0]
    tokens = rows * n_row
    slots = n_row // 2
    row, col = lax.axis_index("row"), lax.axis_index("col")
    core = col % 2
    flags = jnp.stack([row, core, col]).astype(jnp.int32)
    row_bits, col_bits = bits_of(n_row), bits_of(n_col)

    def first_hops(own, x_own, near_first):
        blocks = {0: own}
        for bit in row_bits:
            source = x_own if bit == 1 else own
            if near_first and bit == row_bits[-1]:
                source = after(source, blocks[1], blocks[2])
            blocks[bit] = swap(source, "row", bit)
        return blocks

    def other_hops(blocks, events=(), late=()):
        near, blocks = blocks, dict(blocks)
        for bit in reversed(row_bits[1:]):
            for index in sorted(blocks):
                if index > 0 and index % (2 * bit) == 0:
                    blocks[index | bit] = swap(after(blocks[index], *events), "row", bit)
        for index in sorted(blocks):
            if index > 0 and index % 2 == 0:
                source = after(blocks[index], *(events if index in near else late))
                blocks[index | 1] = swap(source, "row", 1)
        return [blocks[index] for index in range(n_row)]

    groups = 2 if slots % 2 == 0 else 1
    per_group = slots // groups
    count = per_group * rows
    by_group = [range(2 * g * per_group, 2 * (g + 1) * per_group) for g in range(groups)]

    pieces, offsets = [pre_act], [0]
    for bit in reversed(col_bits):
        pieces = pieces + [swap(piece, "col", bit) for piece in pieces]
        offsets = offsets + [offset ^ bit for offset in offsets]

    own = out_grad * token_valid.astype(BF16)[:, None]
    masked = other_hops(first_hops(own, own, True))
    own = after(inputs, masked[-2])

    blocks, totals, received = [], [], []
    for group, indices in enumerate(by_group):
        if group == 1:
            act, slope = gelu_all(
                [after(pieces[0], *totals)] + pieces[1:],
                offsets,
                flags,
                n_row,
                per_group,
                rows,
            )
            masked[-1] = swap(after(masked[-2], act, masked[n_row // 2 + 1]), "row", 1)
            inputs_hops = first_hops(own, after(own, masked[-1]), False)
        base = 2 * group * per_group
        block = arrange(
            [masked[index] for index in indices],
            [
                [lambda core, i=index, b=base: token_place(i, core, per_group) - b]
                for index in indices
            ],
            rows,
            flags,
        )
        blocks.append(block)
        if group == 0:
            first, second = [], [masked[n_row // 2], pieces[1]]
        else:
            first = received
            second = [inputs_hops[bit] for bit in row_bits]
        partial = lax.dot_general(
            after(block, *first), w_down, LAST, preferred_element_type=F32
        )
        total = partial[:count]
        got = swap(after(partial[count:].astype(BF16), *second), "col", 1)
        for bit in col_bits[1:]:
            total = total + got.astype(F32)
            got = swap(total.astype(BF16), "col", bit)
        totals.append(total)
        received.append(got)
    masked_all = arrange(
        [after(blocks[0], total)] + blocks[1:],
        [
            [lambda core, p=p: p for p in range(2 * g * per_group, 2 * (g + 1) * per_group)]
            for g in range(groups)
        ],
        rows,
        flags,
    )
    masked_gram = gram(masked_all)
    inputs_blocks = other_hops(inputs_hops, [partial], [masked_gram])
    hidden_blocks = []
    for group, (total, got) in enumerate(zip(totals, received)):
        if hidden_blocks:
            events = [inputs_blocks[3], inputs_blocks[n_row // 2 + 1]]
            got = after(got, hidden_blocks[-1], masked_gram, *events)
        total = total + got.astype(F32)
        hidden = (total * slope[group * count : (group + 1) * count]).astype(BF16)
        hidden_blocks += [hidden, swap(hidden, "col", 1)]
    square_down = jnp.sum(masked_gram * gram(after(act, hidden)))

    def exchange_place(side, slot, swapped):
        return lambda core: (side ^ (core & swapped)) * slots + turned(slot, slots)

    hidden_all = arrange(
        hidden_blocks,
        [
            [exchange_place(side, g * per_group + k, 1) for k in range(per_group)]
            for g in range(groups)
            for side in range(2)
        ],
        rows,
        flags,
    )

    flag_value = poison[0, 0].astype(F32)
    keep_block = 1.0 - flag_value
    count_term = jnp.where(col == 0, jnp.sum(token_valid.astype(F32)), 0.0)

    model = w_up.shape[0]
    parts = 3 if model % (3 * TILE) == 0 else 1
    step = model // parts
    sums = []
    operand = hidden_all
    for part in range(parts):
        product = lax.dot_general(
            operand, w_up[part * step : (part + 1) * step], LAST, preferred_element_type=F32
        )
        theirs = product[tokens // 2 :].astype(BF16)
        sums.append((product[: tokens // 2], swap(theirs, "row", 1)))
        operand = after(operand, theirs, inputs_blocks[-1])

    inputs_all = arrange(
        [after(inputs_blocks[0], square_down, theirs)] + inputs_blocks[1:],
        [[exchange_place(index % 2, index // 2, 0)] for index in range(n_row)],
        rows,
        flags,
    )
    inputs_gram = gram(inputs_all)
    square_up = jnp.sum(inputs_gram * gram(hidden_all))
    scalars = jnp.stack([count_term, keep_block * (square_down + square_up), flag_value])
    for bit in col_bits:
        scalars = scalars + swap(scalars, "col", bit)
    for bit in row_bits[1:]:
        scalars = scalars + swap(scalars, "row", bit)
    stages = []
    for total, got in sums:
        stages.append([total + after(got, scalars).astype(F32)])
        for bit in row_bits[1:]:
            total = stages[-1][-1]
            split = total.shape[0] // 2
            got = swap(total[split:].astype(BF16), "row", bit)
            stages[-1].append(total[:split] + got.astype(F32))
    scalars = scalars + swap(scalars, "row", 1)
    count_all, square_all, flag_all = scalars[0], jnp.maximum(scalars[1], 0.0), scalars[2]

    token_total = jnp.maximum(count_all, 1.0)
    squares = square_all / (token_total * token_total)
    block_count = float(n_row * n_col)
    estimate = squares * block_count / jnp.maximum(block_count - flag_all, 1.0)
    limit = 0.25 * math.sqrt(
        (w_up.shape[1] * n_row) * (w_up.shape[0] * n_col) / tokens
    )
    clip_factor = jnp.minimum(1.0, limit / jnp.sqrt(estimate + 1e-06))
    scale = keep_block * clip_factor / token_total

    def gradient(left, right, scale):
        product = lax.dot_general(left, right, FIRST, preferred_element_type=F32)
        return (product * scale).astype(BF16)

    grad_down = gradient(act, masked_all, after(scale, *[stage[0] for stage in stages]))
    events = [stage[1] for stage in stages] + [grad_down]
    grad_up = gradient(inputs_all, hidden_all, after(scale, *events))
    input_sum = jnp.concatenate([stage[-1] for stage in stages], axis=1)
    return (input_sum / token_total).astype(BF16), grad_up, grad_down


def solution(mesh):
    placed = (
        P("row", "col"),
        P("col", "row"),
        P("row", "col"),
        P("row"),
        P("row", "col"),
        P("col", "row"),
        P("row", "col"),
    )
    return jax.shard_map(
        on_device,
        mesh=mesh,
        in_specs=placed,
        out_specs=(P("row", "col"), P("col", "row"), P("row", "col")),
        check_vma=False,
    )
```

```python
import math

import jax
import jax.numpy as jnp
from jax import lax
from jax.experimental import pallas as pl
from jax.experimental.pallas import tpu as pltpu
from jax.sharding import PartitionSpec as P

F32 = jnp.float32
BF16 = jnp.bfloat16
LAST = (((1,), (1,)), ((), ()))
FIRST = (((0,), (0,)), ((), ()))
FACTOR = math.sqrt(2.0 / math.pi)
TILE = 256
VMEM_LIMIT = 56 * 1024 * 1024


def swap(value, axis, bit):
    size = lax.axis_size(axis)
    return lax.ppermute(value, axis, [(i, i ^ bit) for i in range(size)])


def bits_of(size):
    return [1 << i for i in range(size.bit_length() - 1)]


def turned(index, size):
    return sum(((index // bit) % 2) * (size // 2 // bit) for bit in bits_of(size))


def call(kernel, grid, in_specs, out_specs, out_shape, moved):
    return pl.pallas_call(
        kernel,
        grid_spec=pltpu.PrefetchScalarGridSpec(
            num_scalar_prefetch=1,
            grid=grid,
            in_specs=in_specs,
            out_specs=out_specs,
        ),
        out_shape=out_shape,
        compiler_params=pltpu.CompilerParams(
            dimension_semantics=("arbitrary",), vmem_limit_bytes=VMEM_LIMIT
        ),
        cost_estimate=pl.CostEstimate(
            flops=1000, bytes_accessed=moved, transcendentals=0
        ),
    )


def whole_index(i, flags):
    return (0, 0)


def column_index(i, flags):
    return (0, i)


def aligned(start):
    return pl.multiple_of(start, 16)


def token_place(index, core, per_group):
    group, k = index // 2 // per_group, index // 2 % per_group
    return (2 * group + (index % 2 ^ core)) * per_group + k


def widest(width, limit):
    return max(tile for tile in range(128, limit + 1, 128) if width % tile == 0)


def gelu_all(pieces, offsets, flags, n_row, per_group, rows):
    width = pieces[0].shape[1]
    per_col = pieces[0].shape[0] // rows
    tokens = n_row * rows
    tile = widest(width, 256)

    def kernel(flags_ref, *refs):
        act_ref, slope_ref = refs[-2:]
        row, core, col = flags_ref[0], flags_ref[1], flags_ref[2]
        for ref, offset in zip(refs[:-2], offsets):
            for part in range(per_col):
                index = row ^ ((col ^ offset) * per_col + part)
                hval = ref[part * rows : (part + 1) * rows, :].astype(F32)
                tanh_part = jnp.tanh(FACTOR * (hval + 0.044715 * hval * hval * hval))
                place = token_place(index, core, per_group)
                act_ref[pl.ds(aligned(place * rows), rows), :] = (
                    0.5 * hval * (1.0 + tanh_part)
                ).astype(BF16)

                @pl.when(index % 2 == core)
                def _():
                    slope_ref[pl.ds(aligned((index // 2) * rows), rows), :] = 0.5 * (
                        1.0 + tanh_part
                    ) + 0.5 * hval * (1.0 - tanh_part * tanh_part) * FACTOR * (
                        1.0 + 3.0 * 0.044715 * hval * hval
                    )

    return call(
        kernel,
        (width // tile,),
        [pl.BlockSpec((piece.shape[0], tile), column_index) for piece in pieces],
        [
            pl.BlockSpec((tokens, tile), column_index),
            pl.BlockSpec((tokens // 2, tile), column_index),
        ],
        [
            jax.ShapeDtypeStruct((tokens, width), BF16),
            jax.ShapeDtypeStruct((tokens // 2, width), F32),
        ],
        24 * tokens * width,
    )(flags, *pieces)


def arrange(pieces, places, rows, flags):
    width = pieces[0].shape[1]
    tokens = sum(piece.shape[0] for piece in pieces)
    tile = widest(width, width // 2)

    def kernel(flags_ref, *refs):
        for ref, blocks in zip(refs, places):
            for k, place in enumerate(blocks):
                start = aligned(place(flags_ref[1]) * rows)
                refs[-1][pl.ds(start, rows), :] = ref[k * rows : (k + 1) * rows, :]

    return call(
        kernel,
        (width // tile,),
        [pl.BlockSpec((piece.shape[0], tile), column_index) for piece in pieces],
        pl.BlockSpec((tokens, tile), column_index),
        jax.ShapeDtypeStruct((tokens, width), BF16),
        6 * tokens * width,
    )(flags, *pieces)


def gram(value):
    return lax.dot_general(value, value, LAST, preferred_element_type=F32)


def after(value, *events):
    return lax.optimization_barrier((value, *events))[0]


def on_device(inputs, pre_act, out_grad, token_valid, poison, w_up, w_down):
    n_row = lax.axis_size("row")
    n_col = lax.axis_size("col")
    rows = inputs.shape[0]
    tokens = rows * n_row
    slots = n_row // 2
    row, col = lax.axis_index("row"), lax.axis_index("col")
    core = col % 2
    flags = jnp.stack([row, core, col]).astype(jnp.int32)
    row_bits, col_bits = bits_of(n_row), bits_of(n_col)

    def first_hops(own, x_own, near_first):
        blocks = {0: own}
        for bit in row_bits:
            source = x_own if bit == 1 else own
            if near_first and bit == row_bits[-1]:
                source = after(source, blocks[1], blocks[2])
            blocks[bit] = swap(source, "row", bit)
        return blocks

    def other_hops(blocks, events=(), late=()):
        near, blocks = blocks, dict(blocks)
        for bit in reversed(row_bits[1:]):
            for index in sorted(blocks):
                if index > 0 and index % (2 * bit) == 0:
                    blocks[index | bit] = swap(after(blocks[index], *events), "row", bit)
        for index in sorted(blocks):
            if index > 0 and index % 2 == 0:
                source = after(blocks[index], *(events if index in near else late))
                blocks[index | 1] = swap(source, "row", 1)
        return [blocks[index] for index in range(n_row)]

    groups = 2 if slots % 2 == 0 else 1
    per_group = slots // groups
    count = per_group * rows
    by_group = [range(2 * g * per_group, 2 * (g + 1) * per_group) for g in range(groups)]

    pieces, offsets = [pre_act], [0]
    for bit in reversed(col_bits):
        pieces = pieces + [swap(piece, "col", bit) for piece in pieces]
        offsets = offsets + [offset ^ bit for offset in offsets]

    own = out_grad * token_valid.astype(BF16)[:, None]
    masked = other_hops(first_hops(own, own, True))
    own = after(inputs, masked[-2])

    blocks, totals, received = [], [], []
    for group, indices in enumerate(by_group):
        if group == 1:
            act, slope = gelu_all(
                [after(pieces[0], *totals)] + pieces[1:],
                offsets,
                flags,
                n_row,
                per_group,
                rows,
            )
            masked[-1] = swap(after(masked[-2], act, masked[n_row // 2 + 1]), "row", 1)
            inputs_hops = first_hops(own, after(own, masked[-1]), False)
        base = 2 * group * per_group
        block = arrange(
            [masked[index] for index in indices],
            [
                [lambda core, i=index, b=base: token_place(i, core, per_group) - b]
                for index in indices
            ],
            rows,
            flags,
        )
        blocks.append(block)
        if group == 0:
            first, second = [], [masked[n_row // 2], pieces[1]]
        else:
            first = received
            second = [inputs_hops[bit] for bit in row_bits]
        partial = lax.dot_general(
            after(block, *first), w_down, LAST, preferred_element_type=F32
        )
        total = partial[:count]
        got = swap(after(partial[count:].astype(BF16), *second), "col", 1)
        for bit in col_bits[1:]:
            total = total + got.astype(F32)
            got = swap(total.astype(BF16), "col", bit)
        totals.append(total)
        received.append(got)
    masked_all = arrange(
        [after(blocks[0], total)] + blocks[1:],
        [
            [lambda core, p=p: p for p in range(2 * g * per_group, 2 * (g + 1) * per_group)]
            for g in range(groups)
        ],
        rows,
        flags,
    )
    masked_gram = gram(masked_all)
    inputs_blocks = other_hops(inputs_hops, [partial], [masked_gram])
    hidden_blocks = []
    for group, (total, got) in enumerate(zip(totals, received)):
        if hidden_blocks:
            events = [inputs_blocks[3], inputs_blocks[n_row // 2 + 1]]
            got = after(got, hidden_blocks[-1], masked_gram, *events)
        total = total + got.astype(F32)
        hidden = (total * slope[group * count : (group + 1) * count]).astype(BF16)
        hidden_blocks += [hidden, swap(hidden, "col", 1)]
    square_down = jnp.sum(masked_gram * gram(after(act, hidden)))

    def exchange_place(side, slot, swapped):
        return lambda core: (side ^ (core & swapped)) * slots + turned(slot, slots)

    hidden_all = arrange(
        hidden_blocks,
        [
            [exchange_place(side, g * per_group + k, 1) for k in range(per_group)]
            for g in range(groups)
            for side in range(2)
        ],
        rows,
        flags,
    )

    flag_value = poison[0, 0].astype(F32)
    keep_block = 1.0 - flag_value
    count_term = jnp.where(col == 0, jnp.sum(token_valid.astype(F32)), 0.0)

    model = w_up.shape[0]
    parts = 3 if model % (3 * TILE) == 0 else 1
    step = model // parts
    sums = []
    operand = hidden_all
    for part in range(parts):
        product = lax.dot_general(
            operand, w_up[part * step : (part + 1) * step], LAST, preferred_element_type=F32
        )
        theirs = product[tokens // 2 :].astype(BF16)
        sums.append((product[: tokens // 2], swap(theirs, "row", 1)))
        operand = after(operand, theirs, inputs_blocks[-1])

    inputs_all = arrange(
        [after(inputs_blocks[0], square_down, theirs)] + inputs_blocks[1:],
        [[exchange_place(index % 2, index // 2, 0)] for index in range(n_row)],
        rows,
        flags,
    )
    inputs_gram = gram(inputs_all)
    square_up = jnp.sum(inputs_gram * gram(hidden_all))
    scalars = jnp.stack([count_term, keep_block * (square_down + square_up), flag_value])
    for bit in col_bits:
        scalars = scalars + swap(scalars, "col", bit)
    col_sums = scalars
    for bit in row_bits[1:]:
        scalars = scalars + swap(scalars, "row", bit)
    stages = []
    for total, got in sums:
        stages.append([total + after(got, col_sums).astype(F32)])
        for bit in row_bits[1:]:
            total = stages[-1][-1]
            split = total.shape[0] // 2
            got = swap(after(total[split:].astype(BF16), scalars), "row", bit)
            stages[-1].append(total[:split] + got.astype(F32))
    scalars = scalars + swap(scalars, "row", 1)
    count_all, square_all, flag_all = scalars[0], jnp.maximum(scalars[1], 0.0), scalars[2]

    token_total = jnp.maximum(count_all, 1.0)
    squares = square_all / (token_total * token_total)
    block_count = float(n_row * n_col)
    estimate = squares * block_count / jnp.maximum(block_count - flag_all, 1.0)
    limit = 0.25 * math.sqrt(
        (w_up.shape[1] * n_row) * (w_up.shape[0] * n_col) / tokens
    )
    clip_factor = jnp.minimum(1.0, limit / jnp.sqrt(estimate + 1e-06))
    scale = keep_block * clip_factor / token_total

    def gradient(left, right, scale):
        product = lax.dot_general(left, right, FIRST, preferred_element_type=F32)
        return (product * scale).astype(BF16)

    grad_down = gradient(act, masked_all, after(scale, *[stage[0] for stage in stages]))
    events = [stage[1] for stage in stages] + [grad_down]
    grad_up = gradient(inputs_all, hidden_all, after(scale, *events))
    input_sum = jnp.concatenate([stage[-1] for stage in stages], axis=1)
    return (input_sum / token_total).astype(BF16), grad_up, grad_down


def solution(mesh):
    placed = (
        P("row", "col"),
        P("col", "row"),
        P("row", "col"),
        P("row"),
        P("row", "col"),
        P("col", "row"),
        P("row", "col"),
    )
    return jax.shard_map(
        on_device,
        mesh=mesh,
        in_specs=placed,
        out_specs=(P("row", "col"), P("col", "row"), P("row", "col")),
        check_vma=False,
    )
```
